32 devices in a mesh: grp: 16 (over z, x, core), tp: 2 (over y).
Axes of the slice: x: 2, y: 2, z: 4, core: 2. Of those that a mesh axis runs over, the one named last changes fastest.
Arguments:
- kv_weight: bfloat16 [8192, 2048], P('tp'), may hold values from -0.0625 to 0.0625
- kv_bias: bfloat16 [2048], P('tp'), may hold values from -3 to 3
- hidden_in: bfloat16 [4, 16, 32, 8192], P(None, 'grp', None, 'tp'), may hold values from -6 to 6
- queries: bfloat16 [4, 16, 32, 8192], P(None, 'grp', None, 'tp'), may hold values from -139 to 139
- res_cache: bfloat16 [16, 16, 128, 2048], P('grp', None, None, 'tp'), may hold values from -6 to 6
- res_len: int32 [16, 16], P('grp'), may hold values from 1 to 128, 1088 in all within a row
- long_cache: bfloat16 [16, 16, 512, 2048], P('grp', None, None, 'tp'), may hold values from -6 to 6
- long_len: int32 [16, 16], replicated, may hold values from 1 to 512, 4096 in all within a row
- long_dest: int32 [16, 16], replicated, may hold values from 0 to 15, each once within a row
Outputs:
- attention_out: bfloat16 [4, 16, 32, 8192], P(None, 'grp', None, 'tp')
The draws below stay inside these ranges and needn't reach their ends.
Inputs may be any that keep to these rules, and one draw needn't show every extreme that they name: `res_len`: each group's lengths sum to 1088, and the largest is 128. `long_len`: each home group's lengths sum to 4096, and the largest is 512. `long_dest`: each row is a permutation of the groups, so every group sends one request to every group and receives one from every group.
All inputs are finite; a program needn't handle non-finite values.
Results may differ from the reference program's by a relative error of at most 0.0051.
Values may be sent and summed in bfloat16 or wider, within the bound.
No kernel may reach another device: no remote copies, remote signals or barrier semaphores. Data moves between devices by JAX's collectives and lax.ppermute only.
A program may use at most 192 MiB of HBM per device.

```python
import math
import jax
import jax.numpy as jnp
import numpy as np
from jax import lax

D = 8192
H = 64
KVH = 8
HS = 128
STEPS = 4
RES = 16
SHORT = 128
LONG = 512
GROUPS = 16
RQ = 32
N_GRP = 16


def draw_queries(key, part):
    rows = RES + GROUPS
    shape = (STEPS, GROUPS, rows, H * HS)
    values = jnp.clip(jax.random.normal(key, shape, jnp.float32), -6.0, 6.0)
    return values.astype(jnp.bfloat16)


def level_of(key, extent, cuts, low, top_value):
    def one(dim, parts):
        steps = jax.random.uniform(jax.random.fold_in(jax.random.fold_in(key, 6), dim), (parts,), jnp.float32, low / len(cuts), top_value / len(cuts))
        return jnp.repeat(jnp.exp(steps), extent[dim] // parts).reshape((-1,) + (1,) * (len(extent) - dim - 1))

    loudness = one(*cuts[0])
    for cut in cuts[1:]:
        loudness = loudness * one(*cut)
    return loudness


def split_up(count, total, bound, lean):
    weights = [(1 << 20) // math.isqrt(rank ** lean) + 1 for rank in range(2, count + 1)]
    surplus, given = total - bound - (count - 1), [1] * (count - 1)
    while surplus > 0:
        movable = [i for i in range(count - 1) if given[i] < bound]
        pool, budget = sum([weights[i] for i in movable]), surplus
        for i in movable:
            addition = min(bound - given[i], max(1, budget * weights[i] // pool), surplus)
            given[i] = given[i] + addition
            surplus = surplus - addition
    return np.array([bound] + given)


def ragged_sizes(stream_key, number_of, total, most, skew):
    if number_of == 2:
        one = jax.random.randint(stream_key, (), max(1, total - most), min(most, total - 1) + 1)
        return jnp.stack([one, total - one])
    tallies = jnp.asarray(split_up(number_of, total, most, skew), jnp.int32)
    pairs = (number_of - 1) // 2
    giver, sink = tallies[1:1 + 2 * pairs:2], tallies[2:2 + 2 * pairs:2]
    slack = jnp.minimum(giver - 1, most - sink)
    moved = jax.random.randint(jax.random.fold_in(stream_key, 1), (pairs,), 0, 1 << 20) % (slack + 1)
    tallies = tallies.at[1:1 + 2 * pairs:2].set(giver - moved).at[2:2 + 2 * pairs:2].set(sink + moved)
    return tallies[jax.random.permutation(jax.random.fold_in(stream_key, 2), number_of)]


def noise(own_key, dims, width, reach, shards=(), kind=jnp.bfloat16):
    entries = jax.random.normal(own_key, dims, jnp.float32) * width
    if len(shards) > 0:
        entries = level_of(own_key, dims, shards, -0.22, 0.18) * entries
    return jnp.clip(entries, min=-reach, max=reach).astype(kind)


def setup_inputs(seed: int = 0) -> dict:
    arg_keys = jax.random.split(jax.random.key(seed), 10)
    kv_weight = noise(arg_keys[0], (D, 2 * KVH * HS), D ** -0.5, 0.0625, ((0, 2),))
    kv_bias = noise(arg_keys[1], (2 * KVH * HS,), 0.5, 3.0, ((0, 2),))
    hidden_in = noise(arg_keys[2], (STEPS, GROUPS, RQ, D), 1.0, 6.0, ((1, 16), (3, 2)))
    queries = draw_queries(jax.random.fold_in(arg_keys[9], 71), 0)
    res_cache = noise(arg_keys[4], (GROUPS, RES, SHORT, 2 * KVH * HS), 1.0, 6.0, ((0, 16), (3, 2)))
    res_len = jax.vmap(lambda own: ragged_sizes(own, RES, (RES + 1) * SHORT // 2, SHORT, 2))(jax.random.split(arg_keys[5], GROUPS)).reshape((GROUPS, RES)).astype(jnp.int32)
    long_cache = noise(arg_keys[6], (GROUPS, GROUPS, LONG, 2 * KVH * HS), 1.0, 6.0, ((0, 16), (3, 2)))
    long_len = jax.vmap(lambda own: ragged_sizes(own, GROUPS, GROUPS * LONG // 2, LONG, 2))(jax.random.split(arg_keys[7], GROUPS)).reshape((GROUPS, GROUPS)).astype(jnp.int32)
    long_dest = jax.vmap(lambda own: jax.random.permutation(own, GROUPS))(jax.random.split(arg_keys[8], GROUPS)).reshape((GROUPS, GROUPS)).astype(jnp.int32)
    return dict(kv_weight=kv_weight, kv_bias=kv_bias, hidden_in=hidden_in, queries=queries, res_cache=res_cache, res_len=res_len, long_cache=long_cache, long_len=long_len, long_dest=long_dest)


ROPE_BASE = 1000000.0
masked_score = -1.0e30


def rotate(keys_raw, positions):
    half_dim = HS // 2
    freqs = jnp.power(jnp.float32(ROPE_BASE), -2.0 * jnp.arange(half_dim, dtype=jnp.float32) / HS)
    angles = positions.astype(jnp.float32)[..., None] * freqs
    cosine = jnp.cos(angles)
    sine = jnp.sin(angles)
    first_half = keys_raw[..., :half_dim]
    second_half = keys_raw[..., half_dim:]
    return jnp.concatenate([first_half * cosine - second_half * sine, second_half * cosine + first_half * sine], axis=-1)


def attend(query, cache, lengths, new_keys, new_values):
    kv_heads = new_keys.shape[2]
    capacity = cache.shape[1]
    cache = cache.reshape(cache.shape[0], capacity, kv_heads, 2 * HS).astype(jnp.float32)
    old_keys = cache[..., :HS]
    old_values = cache[..., HS:]
    query = query.astype(jnp.float32)
    scale = HS ** -0.5
    scores_old = jnp.einsum("sbkqd,bckd->sbkqc", query, old_keys) * scale
    valid = jnp.arange(capacity, dtype=jnp.int32)[None, :] < lengths[:, None]
    scores_old = jnp.where(valid[None, :, None, None, :], scores_old, masked_score)
    scores_new = jnp.einsum("sbkqd,tbkd->sbkqt", query, new_keys.astype(jnp.float32)) * scale
    step_count = new_keys.shape[0]
    causal = jnp.arange(step_count)[None, :] <= jnp.arange(step_count)[:, None]
    scores_new = jnp.where(causal[:, None, None, None, :], scores_new, masked_score)
    highest = jnp.maximum(jnp.max(scores_old, -1), jnp.max(scores_new, -1))[..., None]
    probs_old = jnp.exp(scores_old - highest)
    probs_new = jnp.exp(scores_new - highest)
    total = jnp.sum(probs_old, -1, keepdims=True) + jnp.sum(probs_new, -1, keepdims=True)
    weights_old = (probs_old / total).astype(jnp.bfloat16).astype(jnp.float32)
    weights_new = (probs_new / total).astype(jnp.bfloat16).astype(jnp.float32)
    mixed = jnp.einsum("sbkqc,bckd->sbkqd", weights_old, old_values)
    mixed = mixed + jnp.einsum("sbkqt,tbkd->sbkqd", weights_new, new_values.astype(jnp.float32))
    return mixed.astype(jnp.bfloat16)


def reference(kv_weight, kv_bias, hidden_in, queries, res_cache, res_len, long_cache, long_len, long_dest):
    group_count = N_GRP
    serve_rows = RES + group_count
    q_per_kv = H // KVH

    def one_group(group):
        hidden_rows = lax.dynamic_index_in_dim(hidden_in, group, 1, keepdims=False)
        hidden_rows = hidden_rows.reshape(STEPS * serve_rows, D)
        kv_new = jnp.dot(hidden_rows, kv_weight, preferred_element_type=jnp.float32) + kv_bias.astype(jnp.float32)
        kv_new = kv_new.reshape(STEPS, serve_rows, KVH, 2 * HS)
        matched = (long_dest == group).astype(jnp.int32)
        picked = jnp.argmax(matched, axis=1).astype(jnp.int32)
        len_in = jnp.sum(matched * long_len, axis=1).astype(jnp.int32)
        arrived = long_cache[jnp.arange(group_count, dtype=jnp.int32), picked]
        own_len = lax.dynamic_index_in_dim(res_len, group, 0, keepdims=False).astype(jnp.int32)
        own_cache = lax.dynamic_index_in_dim(res_cache, group, 0, keepdims=False)
        served_len = jnp.concatenate([own_len, len_in])
        positions = served_len[None, :] + jnp.arange(STEPS, dtype=jnp.int32)[:, None]
        new_keys = rotate(kv_new[..., :HS], positions[:, :, None]).astype(jnp.bfloat16)
        new_values = kv_new[..., HS:].astype(jnp.bfloat16)
        query = lax.dynamic_index_in_dim(queries, group, 1, keepdims=False)
        query = query.reshape(STEPS, serve_rows, KVH, q_per_kv, HS)
        staying = attend(query[:, :RES], own_cache, own_len, new_keys[:, :RES], new_values[:, :RES])
        moving = attend(query[:, RES:], arrived, len_in, new_keys[:, RES:], new_values[:, RES:])
        joined = jnp.concatenate([staying, moving], axis=1)
        return joined.reshape(STEPS, serve_rows, H * HS)

    results = lax.map(one_group, jnp.arange(group_count, dtype=jnp.int32))
    return jnp.transpose(results, (1, 0, 2, 3))
```

```python
import jax
import jax.numpy as jnp
from jax import lax
from jax.sharding import PartitionSpec as P

HS = 128


ROPE_BASE = 1000000.0
masked_score = -1e30


def rotate(keys_raw, positions):
    half_dim = HS // 2
    freqs = jnp.power(jnp.float32(ROPE_BASE), -2.0 * jnp.arange(half_dim, dtype=jnp.float32) / HS)
    angles = positions.astype(jnp.float32)[..., None] * freqs
    cosine = jnp.cos(angles)
    sine = jnp.sin(angles)
    first_half = keys_raw[..., :half_dim]
    second_half = keys_raw[..., half_dim:]
    return jnp.concatenate(
        [first_half * cosine - second_half * sine, second_half * cosine + first_half * sine],
        axis=-1,
    )


def attend_old(query, cache, lengths):
    rows, capacity, cols = cache.shape
    kv_heads = cols // (2 * HS)
    cache = cache.reshape(rows, capacity, kv_heads, 2 * HS)
    scores = jnp.einsum(
        "bknd,bckd->bknc", query, cache[..., :HS], preferred_element_type=jnp.float32
    ) * HS ** (-0.5)
    valid = jnp.arange(capacity, dtype=jnp.int32)[None, :] < lengths[:, None]
    scores = jnp.where(valid[:, None, None, :], scores, masked_score)
    highest = jnp.max(scores, -1, keepdims=True)
    probs = jnp.exp(scores - highest)
    total = jnp.sum(probs, -1, keepdims=True)
    weights = (probs / total).astype(jnp.bfloat16)
    mixed = jnp.einsum(
        "bknc,bckd->bknd", weights, cache[..., HS:], preferred_element_type=jnp.float32
    )
    return mixed, (highest + jnp.log(total))[..., 0]


def per_device(
    kv_weight, kv_bias, hidden_in, queries, res_cache, res_len, long_cache, long_len, long_dest
):
    step_count, _, serve_rows, width_part = hidden_in.shape
    kv_cols = kv_bias.shape[0]
    kv_heads = kv_cols // (2 * HS)
    head_count = queries.shape[3] // HS
    per_kv = head_count // kv_heads
    staying = res_cache.shape[1]
    moving = serve_rows - staying
    tp_size = lax.axis_size("tp")
    tp_index = lax.axis_index("tp")
    group_index = lax.axis_index("grp")
    query = queries[:, 0].reshape(step_count, serve_rows, kv_heads, per_kv, HS)
    query = jnp.transpose(query, (1, 2, 0, 3, 4)).reshape(
        serve_rows, kv_heads, step_count * per_kv, HS
    )
    asked = lax.all_to_all(query[staying:], "grp", split_axis=0, concat_axis=0, tiled=True)

    flat_hidden = hidden_in.reshape(step_count * serve_rows, width_part)
    partial = jnp.dot(flat_hidden, kv_weight, preferred_element_type=jnp.float32)
    kv_raw = lax.dynamic_slice_in_dim(partial, tp_index * kv_cols, kv_cols, axis=1)
    for shift in range(1, tp_size):
        other = lax.rem(tp_index + shift, tp_size)
        piece = lax.dynamic_slice_in_dim(partial, other * kv_cols, kv_cols, axis=1)
        kv_raw = kv_raw + lax.ppermute(
            piece, "tp", [(i, (i + shift) % tp_size) for i in range(tp_size)]
        )

    own_dest = lax.dynamic_index_in_dim(long_dest, group_index, 0, keepdims=False)
    home_len = lax.dynamic_index_in_dim(long_len, group_index, 0, keepdims=False)
    mixed, lse = attend_old(asked[own_dest], long_cache[0], home_len)
    back = jnp.argsort(own_dest)
    lse_hi = lse.astype(jnp.bfloat16)
    rest = lse - lse_hi.astype(jnp.float32)
    lse_mid = rest.astype(jnp.bfloat16)
    lse_lo = (rest - lse_mid.astype(jnp.float32)).astype(jnp.bfloat16)
    count = kv_heads * step_count * per_kv
    answer = jnp.concatenate(
        [mixed.astype(jnp.bfloat16).reshape(moving, -1)]
        + [x.reshape(moving, count) for x in (lse_hi, lse_mid, lse_lo)],
        axis=1,
    )[back]
    answer = lax.all_to_all(answer, "grp", split_axis=0, concat_axis=0, tiled=True)
    moved = answer[:, : count * HS].astype(jnp.float32).reshape(moving, kv_heads, -1, HS)
    stats = answer[:, count * HS :].astype(jnp.float32).reshape(moving, 3, kv_heads, -1)
    moved_lse = stats[:, 0] + stats[:, 1] + stats[:, 2]

    kv_raw = kv_raw + kv_bias.astype(jnp.float32)
    kv_raw = kv_raw.reshape(step_count, serve_rows, kv_heads, 2 * HS)
    matched = (long_dest == group_index).astype(jnp.int32)
    len_in = jnp.sum(matched * long_len, axis=1)
    own_len = res_len[0]
    served_len = jnp.concatenate([own_len, len_in])
    positions = served_len[None, :] + jnp.arange(step_count, dtype=jnp.int32)[:, None]
    new_keys = rotate(kv_raw[..., :HS], positions[:, :, None]).astype(jnp.bfloat16)
    new_values = kv_raw[..., HS:].astype(jnp.bfloat16)

    stayed, stayed_lse = attend_old(query[:staying], res_cache[0], own_len)
    old = jnp.concatenate([stayed, moved], axis=0)
    old_lse = jnp.concatenate([stayed_lse, moved_lse], axis=0)
    scores_new = jnp.einsum(
        "bknd,tbkd->bknt", query, new_keys, preferred_element_type=jnp.float32
    ) * HS ** (-0.5)
    causal = jnp.arange(step_count)[None, :] <= (jnp.arange(step_count * per_kv) // per_kv)[:, None]
    scores_new = jnp.where(causal, scores_new, masked_score)
    highest = jnp.maximum(old_lse, jnp.max(scores_new, -1))[..., None]
    share_old = jnp.exp(old_lse[..., None] - highest)
    probs_new = jnp.exp(scores_new - highest)
    total = share_old + jnp.sum(probs_new, -1, keepdims=True)
    weights_new = (probs_new / total).astype(jnp.bfloat16)
    joined = old * (share_old / total) + jnp.einsum(
        "bknt,tbkd->bknd", weights_new, new_values, preferred_element_type=jnp.float32
    )
    joined = joined.astype(jnp.bfloat16).reshape(serve_rows, kv_heads, step_count, per_kv, HS)
    joined = jnp.transpose(joined, (2, 0, 1, 3, 4))
    return joined.reshape(step_count, 1, serve_rows, head_count * HS)


def solution(mesh):
    placed = (
        P("tp", None),
        P("tp"),
        P(None, "grp", None, "tp"),
        P(None, "grp", None, "tp"),
        P("grp", None, None, "tp"),
        P("grp", None),
        P("grp", None, None, "tp"),
        P(),
        P(),
    )
    return jax.shard_map(
        per_device,
        mesh=mesh,
        in_specs=placed,
        out_specs=P(None, "grp", None, "tp"),
        check_vma=False,
    )
```

```python
import functools
import math

import jax
import jax.numpy as jnp
from jax import lax
from jax.experimental import pallas as pl
from jax.experimental.pallas import tpu as pltpu
from jax.sharding import PartitionSpec as P

HS = 128
ROPE_BASE = 1000000.0
masked_score = -1e30
SCALE = HS ** (-0.5)
LOG2E = math.log2(math.e)
STAT = 16
GROUP = 4
MIB = 1 << 20
FULL = 60 * MIB


def each_variant(used, variants, run):
    if variants == 1:
        run(1)
        return
    for v in range(1, variants + 1):
        pl.when(used == v)(functools.partial(run, v))


def cache_copy(cache_ref, buf, sems, m, rows):
    part = pl.ds(0, rows)
    return pltpu.make_async_copy(cache_ref.at[m, part], buf.at[m, part], sems.at[m])


def moving_kernel(
    dest_ref, length_ref, query_ref, cache_ref, out_ref, buf, stats, order, sems, *, kv_heads
):
    count, capacity, _ = cache_ref.shape
    me = lax.axis_index("grp")
    chunk = min(capacity, 128)
    variants = capacity // chunk
    used = [(length_ref[me, m] + chunk - 1) // chunk for m in range(count)]
    place = [jnp.int32(0)] * (variants + 2)
    for v in range(variants, 0, -1):
        place[v - 1] = place[v] + sum((u == v).astype(jnp.int32) for u in used)
    for v in range(variants + 1):
        order[count + v] = place[v]
    for m in range(count):
        at = order[count + used[m]]
        order[count + used[m]] = at + 1
        order[at] = m
    old_body(
        lambda m: dest_ref[me, m],
        lambda i: order[i],
        lambda m: length_ref[me, m],
        lambda slot, begin, end: query_ref[slot, begin:end, :],
        cache_ref, out_ref, buf, stats, sems, kv_heads,
    )


def staying_kernel(len_ref, query_ref, cache_ref, out_ref, buf, stats, turned, sems, *, kv_heads):
    count, rows = out_ref.shape[0], out_ref.shape[1] - STAT

    def query_of(m, begin, end):
        at = pl.ds(pl.multiple_of(m * rows + begin, 8), end - begin)
        return turned[at, :].astype(jnp.bfloat16)

    def same(m):
        return m

    by_request(query_ref, turned, kv_heads, 0, count)
    old_body(
        same, same, lambda m: len_ref[m], query_of, cache_ref, out_ref, buf, stats, sems, kv_heads
    )


def old_body(
    slot_of, member, length_of, query_of, cache_ref, out_ref, buf, stats, sems, kv_heads
):
    count, capacity, _ = cache_ref.shape
    rows = out_ref.shape[1] - STAT
    per = rows // kv_heads
    chunk = min(capacity, 128)
    variants = capacity // chunk
    pair = 2 if kv_heads % 2 == 0 else 1
    def group_chunks(g):
        if variants == 1:
            return 1
        return (length_of(member(g * GROUP)) + chunk - 1) // chunk

    @pl.loop(0, count // GROUP)
    def _(g):
        def start(v):
            for i in range(GROUP):
                cache_copy(cache_ref, buf, sems, member(g * GROUP + i), v * chunk).start()

        each_variant(group_chunks(g), variants, start)

    stats[...] = jnp.zeros_like(stats)
    lane = lax.broadcasted_iota(jnp.int32, (rows, HS), 1)

    def body(g, v):
        length = v * chunk
        members = [member(g * GROUP + i) for i in range(GROUP)]
        for m in members:
            cache_copy(cache_ref, buf, sems, m, length).wait()
        slots = [slot_of(m) for m in members]
        column = lax.broadcasted_iota(jnp.int32, (pair * per, length), 1)
        part = pl.ds(0, length)
        items = [
            (i, [p * pair + j for j in range(pair)])
            for i in range(GROUP)
            for p in range(kv_heads // pair)
        ]
        queries = []
        for i, heads in items:
            own = [query_of(slots[i], h * per, (h + 1) * per) for h in heads]
            if pair == 2:
                zero = jnp.zeros_like(own[0])
                own = [
                    jnp.concatenate(
                        [jnp.concatenate([own[0], zero], 1), jnp.concatenate([zero, own[1]], 1)], 0
                    )
                ]
            queries.append(own[0])

        def columns(i, heads, shift):
            at = [h * 2 * HS + shift for h in heads]
            return jnp.concatenate([buf[members[i], part, c : c + HS] for c in at], 1)

        scores = [
            lax.dot_general(
                query, columns(i, heads, 0), (((1,), (1,)), ((), ())),
                preferred_element_type=jnp.float32,
            )
            for query, (i, heads) in zip(queries, items)
        ]
        scores = [
            jnp.where(column < length_of(members[i]), x, masked_score)
            for x, (i, _) in zip(scores, items)
        ]
        highest = [jnp.max(x, axis=1, keepdims=True) for x in scores]
        probs = [jnp.exp2((x - h) * (SCALE * LOG2E)) for x, h in zip(scores, highest)]
        total = [jnp.sum(x, axis=1, keepdims=True) for x in probs]
        probs = [x.astype(jnp.bfloat16) for x in probs]
        mixed = [
            jnp.dot(x, columns(i, heads, HS), preferred_element_type=jnp.float32)
            for x, (i, heads) in zip(probs, items)
        ]
        mixed = [x * (1.0 / t) for x, t in zip(mixed, total)]
        lses = [h * SCALE + jnp.log(t) for h, t in zip(highest, total)]
        for x, (i, heads) in zip(mixed, items):
            for j, h in enumerate(heads):
                out_ref[slots[i], h * per : (h + 1) * per, :] = x[
                    j * per : (j + 1) * per, j * HS : (j + 1) * HS
                ].astype(jnp.bfloat16)
        table = stats[0:rows, :]
        for i in range(GROUP):
            lse = jnp.concatenate([x for x, (o, _) in zip(lses, items) if o == i], 0)
            table = jnp.where(lane == slots[i], lse, table)
        stats[0:rows, :] = table

    @pl.loop(0, count // GROUP)
    def _(g):
        each_variant(group_chunks(g), variants, functools.partial(body, g))

    turned = stats[...].T
    row = lax.broadcasted_iota(jnp.int32, (STAT, HS), 0)
    for d in range(count):
        whole = jnp.broadcast_to(turned[d : d + 1, :], (STAT, HS))
        high = whole.astype(jnp.bfloat16).astype(jnp.float32)
        rest = whole - high
        middle = rest.astype(jnp.bfloat16).astype(jnp.float32)
        low = rest - middle
        terms = jnp.where(row == 0, high, jnp.where(row == 1, middle, jnp.where(row == 2, low, 0.0)))
        out_ref[d, rows : rows + STAT, :] = terms.astype(jnp.bfloat16)


def by_request(query_ref, scratch, kv_heads, first, count):
    steps, _, _, cols = query_ref.shape
    per_kv = cols // HS // kv_heads
    rows = steps * cols // HS
    for k in range(kv_heads):
        for s in range(steps):
            for q in range(per_kv):
                h = k * per_kv + q
                tile = query_ref[s, 0, first : first + count, h * HS : (h + 1) * HS].astype(jnp.float32)
                scratch[pl.ds((k * steps + s) * per_kv + q, count, stride=rows), :] = tile


def turn_kernel(query_ref, out_ref, arrived, scratch, turned, in_sems, out_sems, *, kv_heads, first):
    count, rows, _ = out_ref.shape
    per = rows // kv_heads
    width = query_ref.shape[3] // kv_heads
    own = pl.ds(first, count)

    def into(k):
        lanes = pl.ds(k * width, width)
        return pltpu.make_async_copy(
            query_ref.at[:, :, own, lanes], arrived.at[k], in_sems.at[k]
        )

    def outof(k):
        return pltpu.make_async_copy(
            turned.at[k], out_ref.at[:, pl.ds(k * per, per), :], out_sems.at[k]
        )

    for k in range(kv_heads):
        into(k).start()
    for k in range(kv_heads):
        into(k).wait()
        by_request(arrived.at[k], scratch, 1, 0, count)
        turned[k] = scratch[...].astype(jnp.bfloat16).reshape(count, per, HS)
        outof(k).start()
    for k in range(kv_heads):
        outof(k).wait()


def turn(queries, first, kv_heads):
    steps, _, serve, cols = queries.shape
    count, width = serve - first, cols // kv_heads
    per = steps * width // HS
    return pl.pallas_call(
        functools.partial(turn_kernel, kv_heads=kv_heads, first=first),
        out_shape=jax.ShapeDtypeStruct((count, kv_heads * per, HS), jnp.bfloat16),
        in_specs=[pl.BlockSpec(memory_space=pltpu.HBM)],
        out_specs=pl.BlockSpec(memory_space=pltpu.HBM),
        scratch_shapes=[
            pltpu.VMEM((kv_heads, steps, 1, count, width), jnp.bfloat16),
            pltpu.VMEM((count * per, HS), jnp.float32),
            pltpu.VMEM((kv_heads, count, per, HS), jnp.bfloat16),
            pltpu.SemaphoreType.DMA((kv_heads,)),
            pltpu.SemaphoreType.DMA((kv_heads,)),
        ],
        compiler_params=pltpu.CompilerParams(vmem_limit_bytes=FULL),
        cost_estimate=pl.CostEstimate(flops=MIB, bytes_accessed=MIB, transcendentals=0),
        name="turn",
    )(queries)


def project_kernel(index_ref, hidden_ref, weight_ref, out_ref):
    del index_ref
    out_ref[0] = jnp.dot(hidden_ref[...], weight_ref[...], preferred_element_type=jnp.float32)


def project(hidden, weight, kv_cols, tp_size, tp_index, first, pieces):
    rows, depth = hidden.shape
    width = min(kv_cols, 256)
    blocks = kv_cols // width
    return pl.pallas_call(
        project_kernel,
        out_shape=jax.ShapeDtypeStruct((pieces, rows, kv_cols), jnp.float32),
        grid_spec=pltpu.PrefetchScalarGridSpec(
            num_scalar_prefetch=1,
            grid=(pieces, blocks),
            in_specs=[
                pl.BlockSpec((rows, depth), lambda j, c, index: (0, 0)),
                pl.BlockSpec(
                    (depth, width),
                    lambda j, c, index: (0, lax.rem(index[0] + first + j, tp_size) * blocks + c),
                ),
            ],
            out_specs=pl.BlockSpec((1, rows, width), lambda j, c, index: (j, 0, c)),
        ),
        compiler_params=pltpu.CompilerParams(vmem_limit_bytes=FULL),
        cost_estimate=pl.CostEstimate(
            flops=2 * rows * depth * kv_cols * pieces,
            bytes_accessed=depth * kv_cols * pieces * 2,
            transcendentals=0,
        ),
        name="project",
    )(tp_index.reshape(1), hidden, weight)


def old_call(kernel, scalars, query, cache, rows, scratch, limit, name):
    count, capacity, _ = cache.shape
    smem, vmem = pl.BlockSpec(memory_space=pltpu.SMEM), pl.BlockSpec(memory_space=pltpu.VMEM)
    return pl.pallas_call(
        kernel,
        out_shape=jax.ShapeDtypeStruct((count, rows + STAT, HS), jnp.bfloat16),
        in_specs=[smem] * len(scalars) + [vmem, pl.BlockSpec(memory_space=pltpu.HBM)],
        out_specs=vmem,
        scratch_shapes=[
            pltpu.VMEM(cache.shape, jnp.bfloat16),
            pltpu.VMEM((128, HS), jnp.float32),
            scratch,
            pltpu.SemaphoreType.DMA((count,)),
        ],
        compiler_params=pltpu.CompilerParams(vmem_limit_bytes=limit),
        cost_estimate=pl.CostEstimate(
            flops=count * rows * capacity * HS * 8,
            bytes_accessed=cache.size * 2,
            transcendentals=count * rows * capacity,
        ),
        name=name,
    )(*scalars, query, cache)


def old_lse(stat):
    return stat[:, 0, :] + stat[:, 1, :] + stat[:, 2, :]


def merge_tiles(old, share, new_of, put, steps, per_kv, kv_heads, count, heads):
    rows = kv_heads * steps * per_kv
    for k in heads:
        for s in range(steps):
            for q in range(per_kv):
                c = (k * steps + s) * per_kv + q
                before = old[pl.ds(c, count, stride=rows), :]
                new = new_of(s, k * per_kv + q)
                put(s, k * per_kv + q, new + share[:, c : c + 1] * (before - new))


def new_kernel(
    query_ref, mine_ref, other_ref, bias_ref, cos_ref, sin_ref, old_ref, out_ref, lse_ref, scratch,
    *, kv_heads, per_kv, staying,
):
    steps, _, serve, _ = query_ref.shape
    rows = old_ref.shape[1] - STAT
    scratch[...] = old_ref[:, 0:rows, :].astype(jnp.float32).reshape(staying * rows, HS)
    raw = mine_ref[...]
    for i in range(other_ref.shape[0]):
        raw = raw + other_ref[i]
    raw = raw + bias_ref[...].astype(jnp.float32)
    total_rows = steps * serve
    request = lax.broadcasted_iota(jnp.int32, (serve, total_rows), 0)
    column = lax.broadcasted_iota(jnp.int32, (serve, total_rows), 1)
    lane = lax.broadcasted_iota(jnp.int32, (serve, HS), 1)
    lse_all = jnp.zeros((serve, HS), jnp.float32)
    for k in range(kv_heads):
        keys = raw[:, k * 2 * HS : k * 2 * HS + HS]
        keys = keys * cos_ref[...] + pltpu.roll(keys, HS // 2, 1) * sin_ref[...]
        keys = keys.astype(jnp.bfloat16)
        values = raw[:, k * 2 * HS + HS : (k + 1) * 2 * HS].astype(jnp.bfloat16)
        for s in range(steps):
            heads = [k * per_kv + q for q in range(per_kv)]
            query = jnp.concatenate([query_ref[s, 0, :, h * HS : (h + 1) * HS] for h in heads], 0)
            scores = lax.dot_general(
                query, keys, (((1,), (1,)), ((), ())), preferred_element_type=jnp.float32
            )
            seen = column == request
            for t in range(1, s + 1):
                seen = seen | (column == request + t * serve)
            scores = jnp.where(jnp.concatenate([seen] * per_kv, 0), scores, masked_score)
            highest = jnp.max(scores, axis=1, keepdims=True)
            probs = jnp.exp2((scores - highest) * (SCALE * LOG2E))
            total = jnp.sum(probs, axis=1, keepdims=True)
            mixed = jnp.dot(probs.astype(jnp.bfloat16), values, preferred_element_type=jnp.float32)
            mixed = mixed * (1.0 / total)
            lse = highest * SCALE + jnp.log(total)
            for q, h in enumerate(heads):
                c = (k * steps + s) * per_kv + q
                lse_all = jnp.where(lane == c, lse[q * serve : (q + 1) * serve], lse_all)
                out_ref[s, 0, :, h * HS : (h + 1) * HS] = mixed[
                    q * serve : (q + 1) * serve
                ].astype(jnp.bfloat16)
    lse_ref[...] = lse_all

    def put(s, h, value):
        out_ref[s, 0, 0:staying, h * HS : (h + 1) * HS] = value.astype(jnp.bfloat16)

    def new_of(s, h):
        return out_ref[s, 0, 0:staying, h * HS : (h + 1) * HS].astype(jnp.float32)

    stat = old_lse(old_ref[:, rows : rows + STAT, :].astype(jnp.float32))
    share = 1.0 / (1.0 + jnp.exp(lse_all[0:staying] - stat))
    merge_tiles(
        scratch, share, new_of, put, steps, per_kv, kv_heads, staying, range(kv_heads)
    )


def join_kernel(old_ref, new_ref, lse_ref, out_ref, arrived, scratch, merged, in_sem, out_sems, *, kv_heads, first):
    steps = new_ref.shape[0]
    count, rows = old_ref.shape[0], old_ref.shape[1] - STAT
    width = new_ref.shape[3] // kv_heads
    own = pl.ds(first, count)
    into = pltpu.make_async_copy(new_ref.at[:, :, own], arrived, in_sem)

    def outof(k):
        lanes = pl.ds(k * width, width)
        return pltpu.make_async_copy(
            merged.at[:, :, :, lanes], out_ref.at[:, :, own, lanes], out_sems.at[k]
        )

    into.start()
    scratch[...] = old_ref[:, 0:rows, :].astype(jnp.float32).reshape(count * rows, HS)
    stat = old_lse(old_ref[:, rows : rows + STAT, :].astype(jnp.float32))
    share = 1.0 / (1.0 + jnp.exp(lse_ref[first : first + count, :] - stat))
    into.wait()

    def put(s, h, value):
        merged[s, 0, :, h * HS : (h + 1) * HS] = value.astype(jnp.bfloat16)

    def new_of(s, h):
        return arrived[s, 0, :, h * HS : (h + 1) * HS].astype(jnp.float32)

    for k in range(kv_heads):
        merge_tiles(scratch, share, new_of, put, steps, width // HS, kv_heads, count, [k])
        outof(k).start()
    for k in range(kv_heads):
        outof(k).wait()


def per_device(
    kv_weight, kv_bias, hidden_in, queries, res_cache, res_len, long_cache, long_len, long_dest
):
    step_count, _, serve_rows, width_part = hidden_in.shape
    kv_cols = kv_bias.shape[0]
    kv_heads = kv_cols // (2 * HS)
    query_cols = queries.shape[3]
    head_count = query_cols // HS
    per_kv = head_count // kv_heads
    staying = res_cache.shape[1]
    moving = serve_rows - staying
    rows = head_count * step_count
    tp_size = lax.axis_size("tp")
    tp_index = lax.axis_index("tp")
    group_index = lax.axis_index("grp")
    asked = lax.all_to_all(
        turn(queries, staying, kv_heads), "grp", split_axis=0, concat_axis=0, tiled=True
    )

    flat_hidden = hidden_in.reshape(step_count * serve_rows, width_part)
    pieces = project(flat_hidden, kv_weight, kv_cols, tp_size, tp_index, 1, tp_size - 1)
    others = jnp.stack(
        [
            lax.ppermute(pieces[j], "tp", [(i, (i + j + 1) % tp_size) for i in range(tp_size)])
            for j in range(tp_size - 1)
        ]
    )
    mine = project(flat_hidden, kv_weight, kv_cols, tp_size, tp_index, 0, 1)[0]

    answer = old_call(
        functools.partial(moving_kernel, kv_heads=kv_heads),
        [long_dest, long_len],
        asked,
        long_cache[0],
        rows,
        pltpu.SMEM((moving + 8,), jnp.int32),
        48 * MIB,
        "moving_old",
    )
    answer, others, mine = lax.optimization_barrier((answer, others, mine))
    answer = lax.all_to_all(answer, "grp", split_axis=0, concat_axis=0, tiled=True)

    own_len = res_len[0]
    stayed = old_call(
        functools.partial(staying_kernel, kv_heads=kv_heads),
        [own_len],
        queries,
        res_cache[0],
        rows,
        pltpu.VMEM((staying * rows, HS), jnp.float32),
        58 * MIB,
        "staying_old",
    )
    matched = (long_dest == group_index).astype(jnp.int32)
    len_in = jnp.sum(matched * long_len, axis=1)
    served_len = jnp.concatenate([own_len, len_in])
    positions = served_len[None, :] + jnp.arange(step_count, dtype=jnp.int32)[:, None]
    half = HS // 2
    freqs = jnp.power(jnp.float32(ROPE_BASE), -2.0 * jnp.arange(half, dtype=jnp.float32) / HS)
    angles = positions.reshape(-1, 1).astype(jnp.float32) * freqs
    cosine, sine = jnp.cos(angles), jnp.sin(angles)
    cosine = jnp.concatenate([cosine, cosine], 1)
    sine = jnp.concatenate([-sine, sine], 1)

    out_shape = jax.ShapeDtypeStruct((step_count, 1, serve_rows, query_cols), jnp.bfloat16)
    fresh, lse = pl.pallas_call(
        functools.partial(new_kernel, kv_heads=kv_heads, per_kv=per_kv, staying=staying),
        out_shape=(out_shape, jax.ShapeDtypeStruct((serve_rows, HS), jnp.float32)),
        in_specs=[pl.BlockSpec(memory_space=pltpu.VMEM)] * 7,
        out_specs=(pl.BlockSpec(memory_space=pltpu.VMEM),) * 2,
        scratch_shapes=[pltpu.VMEM((staying * rows, HS), jnp.float32)],
        compiler_params=pltpu.CompilerParams(vmem_limit_bytes=24 * MIB),
        cost_estimate=pl.CostEstimate(
            flops=serve_rows * rows * step_count * serve_rows * HS * 4,
            bytes_accessed=8 * MIB,
            transcendentals=serve_rows * rows * step_count * serve_rows,
        ),
        name="new_part",
    )(queries, mine, others, kv_bias.reshape(1, kv_cols), cosine, sine, stayed)

    hbm, vmem = pl.BlockSpec(memory_space=pltpu.HBM), pl.BlockSpec(memory_space=pltpu.VMEM)
    part = (step_count, 1, moving, query_cols)
    return pl.pallas_call(
        functools.partial(join_kernel, kv_heads=kv_heads, first=staying),
        out_shape=out_shape,
        in_specs=[vmem, hbm, vmem],
        out_specs=hbm,
        scratch_shapes=[
            pltpu.VMEM(part, jnp.bfloat16),
            pltpu.VMEM((moving * rows, HS), jnp.float32),
            pltpu.VMEM(part, jnp.bfloat16),
            pltpu.SemaphoreType.DMA,
            pltpu.SemaphoreType.DMA((kv_heads,)),
        ],
        input_output_aliases={1: 0},
        compiler_params=pltpu.CompilerParams(vmem_limit_bytes=32 * MIB),
        cost_estimate=pl.CostEstimate(flops=MIB, bytes_accessed=2 * MIB, transcendentals=0),
        name="join",
    )(answer, fresh, lse)


def solution(mesh):
    placed = (
        P("tp", None),
        P("tp"),
        P(None, "grp", None, "tp"),
        P(None, "grp", None, "tp"),
        P("grp", None, None, "tp"),
        P("grp", None),
        P("grp", None, None, "tp"),
        P(),
        P(),
    )
    return jax.shard_map(
        per_device,
        mesh=mesh,
        in_specs=placed,
        out_specs=P(None, "grp", None, "tp"),
        check_vma=False,
    )
```

```python
import functools
import math

import jax
import jax.numpy as jnp
from jax import lax
from jax.experimental import pallas as pl
from jax.experimental.pallas import tpu as pltpu
from jax.sharding import PartitionSpec as P

HS = 128
ROPE_BASE = 1000000.0
masked_score = -1e30
SCALE = HS ** (-0.5)
LOG2E = math.log2(math.e)
STAT = 8
GROUP = 4
MIB = 1 << 20
FULL = 60 * MIB


def cache_copy(cache_ref, buf, sems, m, rows):
    part = pl.ds(0, rows)
    return pltpu.make_async_copy(cache_ref.at[m, part], buf.at[m, part], sems.at[m])


def moving_kernel(
    dest_ref, length_ref, query_ref, cache_ref, out_ref,
    buf, order, answers, in_sems, out_sems, *, kv_heads,
):
    count, capacity, _ = cache_ref.shape
    me = lax.axis_index("grp")
    chunk = min(capacity, 128)
    variants = capacity // chunk
    used = [(length_ref[me, m] + chunk - 1) // chunk for m in range(count)]
    place = jnp.int32(0)
    for v in range(1, variants + 1):
        order[count + v] = place
        place = place + sum((u == v).astype(jnp.int32) for u in used)
    for m in range(count):
        at = order[count + used[m]]
        order[count + used[m]] = at + 1
        order[at] = m

    def leave(slot):
        return pltpu.make_async_copy(answers.at[slot], out_ref.at[slot], out_sems.at[slot])

    old_body(
        lambda m: dest_ref[me, m],
        lambda i: order[i],
        lambda m: length_ref[me, m],
        lambda slot, begin, end: query_ref[slot, begin:end, :],
        cache_ref, answers, buf, in_sems, kv_heads, lambda slot: leave(slot).start(),
    )

    @pl.loop(0, count)
    def _(slot):
        leave(slot).wait()


def staying_kernel(len_ref, query_ref, cache_ref, out_ref, buf, turned, sems, *, kv_heads):
    count, rows = out_ref.shape[0], out_ref.shape[1] - STAT

    steps, per = query_ref.shape[0], rows // kv_heads

    def same(m):
        return m

    for k in range(kv_heads):
        turned[:, k * per : (k + 1) * per, :] = by_request(
            lambda s, q: query_ref[s, 0, 0:count, pl.ds((k * per // steps + q) * HS, HS)],
            steps, per // steps,
        )
    old_body(
        same, same, lambda m: len_ref[m], lambda m, begin, end: turned[m, begin:end, :],
        cache_ref, out_ref, buf, sems, kv_heads, lambda slot: None,
    )


def stat_rows(lses):
    rows = lses[0].shape[0]
    same = lax.broadcasted_iota(jnp.int32, (rows, HS), 0) == lax.broadcasted_iota(
        jnp.int32, (rows, HS), 1
    )
    row = lax.broadcasted_iota(jnp.int32, (STAT, HS), 0)
    result = []
    for lse in lses:
        turned = jnp.sum(jnp.where(same, lse, 0.0), axis=0, keepdims=True)
        whole = jnp.broadcast_to(turned, (STAT, HS))
        high = whole.astype(jnp.bfloat16).astype(jnp.float32)
        rest = whole - high
        middle = rest.astype(jnp.bfloat16).astype(jnp.float32)
        terms = jnp.where(row == 0, high, jnp.where(row == 1, middle, rest - middle))
        result.append(jnp.where(row < 3, terms, 0.0).astype(jnp.bfloat16))
    return result


def old_body(slot_of, member, length_of, query_of, cache_ref, out_ref, buf, sems, kv_heads, done):
    count, capacity, _ = cache_ref.shape
    rows = out_ref.shape[1] - STAT
    per = rows // kv_heads
    chunk = min(capacity, 128)
    variants = capacity // chunk
    pair = 2 if kv_heads % 2 == 0 else 1
    part_size = [GROUP]

    def run(act):
        def one(first, size):
            if variants == 1:
                act(first, size, 1)
                return
            used = (length_of(member(first + size - 1)) + chunk - 1) // chunk
            for v in range(1, variants + 1):
                pl.when(used == v)(functools.partial(act, first, size, v))

        @pl.loop(0, count // GROUP - 1)
        def _(g):
            one(g * GROUP, GROUP)

        first = count - GROUP
        for size in part_size:
            one(first, size)
            first += size

    def start(first, size, v):
        for i in range(size):
            cache_copy(cache_ref, buf, sems, member(first + i), v * chunk).start()

    def body(first, size, v):
        length = v * chunk
        members = [member(first + i) for i in range(size)]
        for m in members:
            cache_copy(cache_ref, buf, sems, m, length).wait()
        slots = [slot_of(m) for m in members]
        column = lax.broadcasted_iota(jnp.int32, (pair * per, length), 1)
        part = pl.ds(0, length)
        items = [
            (i, [p * pair + j for j in range(pair)])
            for i in range(size)
            for p in range(kv_heads // pair)
        ]
        queries = []
        for i, heads in items:
            own = [query_of(slots[i], h * per, (h + 1) * per) for h in heads]
            if pair == 2:
                zero = jnp.zeros_like(own[0])
                own = [
                    jnp.concatenate(
                        [jnp.concatenate([own[0], zero], 1), jnp.concatenate([zero, own[1]], 1)], 0
                    )
                ]
            queries.append(own[0])

        def columns(i, heads, shift):
            at = [h * 2 * HS + shift for h in heads]
            return jnp.concatenate([buf[members[i], part, c : c + HS] for c in at], 1)

        scores = [
            lax.dot_general(
                query, columns(i, heads, 0), (((1,), (1,)), ((), ())),
                preferred_element_type=jnp.float32,
            )
            for query, (i, heads) in zip(queries, items)
        ]
        scores = [
            jnp.where(column < length_of(members[i]), x, masked_score)
            for x, (i, _) in zip(scores, items)
        ]
        highest = [jnp.max(x, axis=1, keepdims=True) for x in scores]
        probs = [jnp.exp2((x - h) * (SCALE * LOG2E)) for x, h in zip(scores, highest)]
        total = [jnp.sum(x, axis=1, keepdims=True) for x in probs]
        probs = [x.astype(jnp.bfloat16) for x in probs]
        mixed = [
            jnp.dot(x, columns(i, heads, HS), preferred_element_type=jnp.float32)
            for x, (i, heads) in zip(probs, items)
        ]
        mixed = [x * (1.0 / t) for x, t in zip(mixed, total)]
        lses = [h * SCALE + jnp.log(t) for h, t in zip(highest, total)]
        terms = stat_rows(
            [
                jnp.concatenate([x for x, (o, _) in zip(lses, items) if o == i], 0)
                for i in range(size)
            ]
        )
        for x, (i, heads) in zip(mixed, items):
            for j, h in enumerate(heads):
                out_ref[slots[i], h * per : (h + 1) * per, :] = x[
                    j * per : (j + 1) * per, j * HS : (j + 1) * HS
                ].astype(jnp.bfloat16)
        for i in range(size):
            out_ref[slots[i], rows : rows + STAT, :] = terms[i]
            done(slots[i])

    run(start)
    run(body)


def by_request(tile_of, steps, per_kv):
    tiles = [tile_of(s, q) for s in range(steps) for q in range(per_kv)]
    return jnp.swapaxes(jnp.stack(tiles, 0), 0, 1)


def turn_kernel(query_ref, out_ref, arrived, turned, in_sems, out_sems, *, kv_heads, first):
    count, rows, _ = out_ref.shape
    steps = query_ref.shape[0]
    per = rows // kv_heads
    width = query_ref.shape[3] // kv_heads
    own = pl.ds(first, count)

    def into(k):
        lanes = pl.ds(k * width, width)
        return pltpu.make_async_copy(
            query_ref.at[:, :, own, lanes], arrived.at[k], in_sems.at[k]
        )

    def outof(k):
        return pltpu.make_async_copy(
            turned.at[k], out_ref.at[:, pl.ds(k * per, per), :], out_sems.at[k]
        )

    for k in range(kv_heads):
        into(k).start()
    for k in range(kv_heads):
        into(k).wait()
        turned[k] = by_request(
            lambda s, q: arrived[k, s, 0, :, q * HS : (q + 1) * HS], steps, per // steps
        )
        outof(k).start()
    for k in range(kv_heads):
        outof(k).wait()


def turn(queries, first, kv_heads):
    steps, _, serve, cols = queries.shape
    count, width = serve - first, cols // kv_heads
    per = steps * width // HS
    return pl.pallas_call(
        functools.partial(turn_kernel, kv_heads=kv_heads, first=first),
        out_shape=jax.ShapeDtypeStruct((count, kv_heads * per, HS), jnp.bfloat16),
        in_specs=[pl.BlockSpec(memory_space=pltpu.HBM)],
        out_specs=pl.BlockSpec(memory_space=pltpu.HBM),
        scratch_shapes=[
            pltpu.VMEM((kv_heads, steps, 1, count, width), jnp.bfloat16),
            pltpu.VMEM((kv_heads, count, per, HS), jnp.bfloat16),
            pltpu.SemaphoreType.DMA((kv_heads,)),
            pltpu.SemaphoreType.DMA((kv_heads,)),
        ],
        compiler_params=pltpu.CompilerParams(vmem_limit_bytes=FULL),
        cost_estimate=pl.CostEstimate(flops=MIB, bytes_accessed=MIB, transcendentals=0),
        name="turn",
    )(queries)


def project_kernel(index_ref, hidden_ref, weight_ref, out_ref):
    del index_ref
    out_ref[0] = jnp.dot(hidden_ref[...], weight_ref[...], preferred_element_type=jnp.float32)


def project(hidden, weight, kv_cols, tp_size, tp_index, first, pieces):
    rows, depth = hidden.shape
    width = min(kv_cols, 256)
    blocks = kv_cols // width
    return pl.pallas_call(
        project_kernel,
        out_shape=jax.ShapeDtypeStruct((pieces, rows, kv_cols), jnp.float32),
        grid_spec=pltpu.PrefetchScalarGridSpec(
            num_scalar_prefetch=1,
            grid=(pieces, blocks),
            in_specs=[
                pl.BlockSpec((rows, depth), lambda j, c, index: (0, 0)),
                pl.BlockSpec(
                    (depth, width),
                    lambda j, c, index: (0, lax.rem(index[0] + first + j, tp_size) * blocks + c),
                ),
            ],
            out_specs=pl.BlockSpec((1, rows, width), lambda j, c, index: (j, 0, c)),
        ),
        compiler_params=pltpu.CompilerParams(vmem_limit_bytes=FULL),
        cost_estimate=pl.CostEstimate(
            flops=2 * rows * depth * kv_cols * pieces,
            bytes_accessed=depth * kv_cols * pieces * 2,
            transcendentals=0,
        ),
        name="project",
    )(tp_index.reshape(1), hidden, weight)


def old_call(kernel, scalars, query, cache, rows, scratch, out_space, limit, name):
    count, capacity, _ = cache.shape
    smem, vmem = pl.BlockSpec(memory_space=pltpu.SMEM), pl.BlockSpec(memory_space=pltpu.VMEM)
    return pl.pallas_call(
        kernel,
        out_shape=jax.ShapeDtypeStruct((count, rows + STAT, HS), jnp.bfloat16),
        in_specs=[smem] * len(scalars) + [vmem, pl.BlockSpec(memory_space=pltpu.HBM)],
        out_specs=pl.BlockSpec(memory_space=out_space),
        scratch_shapes=[pltpu.VMEM(cache.shape, jnp.bfloat16)] + scratch,
        compiler_params=pltpu.CompilerParams(vmem_limit_bytes=limit),
        cost_estimate=pl.CostEstimate(
            flops=count * rows * capacity * HS * 8,
            bytes_accessed=cache.size * 2,
            transcendentals=count * rows * capacity,
        ),
        name=name,
    )(*scalars, query, cache)


def old_lse(stat):
    return stat[:, 0, :] + stat[:, 1, :] + stat[:, 2, :]


def merge_head(old_ref, share, new_of, put, steps, per_kv, k):
    per = steps * per_kv
    old = jnp.swapaxes(old_ref[:, k * per : (k + 1) * per, :], 0, 1).astype(jnp.float32)
    for s in range(steps):
        for q in range(per_kv):
            at = s * per_kv + q
            c = k * per + at
            new = new_of(s, k * per_kv + q)
            put(s, k * per_kv + q, new + share[:, c : c + 1] * (old[at] - new))


def new_kernel(
    query_ref, mine_ref, other_ref, bias_ref, cos_ref, sin_ref, old_ref, out_ref, lse_ref,
    *, kv_heads, per_kv, staying,
):
    steps, _, serve, _ = query_ref.shape
    rows = old_ref.shape[1] - STAT
    raw = mine_ref[...]
    for i in range(other_ref.shape[0]):
        raw = raw + other_ref[i]
    raw = raw + bias_ref[...].astype(jnp.float32)
    total_rows = steps * serve
    request = lax.broadcasted_iota(jnp.int32, (serve, total_rows), 0)
    column = lax.broadcasted_iota(jnp.int32, (serve, total_rows), 1)
    lane = lax.broadcasted_iota(jnp.int32, (serve, HS), 1)
    lse_all = jnp.zeros((serve, HS), jnp.float32)
    for k in range(kv_heads):
        keys = raw[:, k * 2 * HS : k * 2 * HS + HS]
        keys = keys * cos_ref[...] + pltpu.roll(keys, HS // 2, 1) * sin_ref[...]
        keys = keys.astype(jnp.bfloat16)
        values = raw[:, k * 2 * HS + HS : (k + 1) * 2 * HS].astype(jnp.bfloat16)
        for s in range(steps):
            heads = [k * per_kv + q for q in range(per_kv)]
            query = jnp.concatenate([query_ref[s, 0, :, h * HS : (h + 1) * HS] for h in heads], 0)
            scores = lax.dot_general(
                query, keys, (((1,), (1,)), ((), ())), preferred_element_type=jnp.float32
            )
            seen = column == request
            for t in range(1, s + 1):
                seen = seen | (column == request + t * serve)
            scores = jnp.where(jnp.concatenate([seen] * per_kv, 0), scores, masked_score)
            highest = jnp.max(scores, axis=1, keepdims=True)
            probs = jnp.exp2((scores - highest) * (SCALE * LOG2E))
            total = jnp.sum(probs, axis=1, keepdims=True)
            mixed = jnp.dot(probs.astype(jnp.bfloat16), values, preferred_element_type=jnp.float32)
            mixed = mixed * (1.0 / total)
            lse = highest * SCALE + jnp.log(total)
            for q, h in enumerate(heads):
                c = (k * steps + s) * per_kv + q
                lse_all = jnp.where(lane == c, lse[q * serve : (q + 1) * serve], lse_all)
                out_ref[s, 0, :, h * HS : (h + 1) * HS] = mixed[
                    q * serve : (q + 1) * serve
                ].astype(jnp.bfloat16)
    lse_ref[...] = lse_all

    def put(s, h, value):
        out_ref[s, 0, 0:staying, h * HS : (h + 1) * HS] = value.astype(jnp.bfloat16)

    def new_of(s, h):
        return out_ref[s, 0, 0:staying, h * HS : (h + 1) * HS].astype(jnp.float32)

    stat = old_lse(old_ref[:, rows : rows + STAT, :].astype(jnp.float32))
    share = 1.0 / (1.0 + jnp.exp(lse_all[0:staying] - stat))
    for k in range(kv_heads):
        merge_head(old_ref, share, new_of, put, steps, per_kv, k)


def join_kernel(old_ref, new_ref, lse_ref, out_ref, arrived, merged, in_sems, out_sems, *, kv_heads, first):
    steps = new_ref.shape[0]
    count, rows = old_ref.shape[0], old_ref.shape[1] - STAT
    width = new_ref.shape[3] // kv_heads
    own = pl.ds(first, count)

    def into(k):
        lanes = pl.ds(k * width, width)
        return pltpu.make_async_copy(new_ref.at[:, :, own, lanes], arrived.at[k], in_sems.at[k])

    def outof(k):
        lanes = pl.ds(k * width, width)
        return pltpu.make_async_copy(merged.at[k], out_ref.at[:, :, own, lanes], out_sems.at[k])

    for k in range(kv_heads):
        into(k).start()
    stat = old_lse(old_ref[:, rows : rows + STAT, :].astype(jnp.float32))
    share = 1.0 / (1.0 + jnp.exp(lse_ref[first : first + count, :] - stat))
    for k in range(kv_heads):
        base = k * width

        def put(s, h, value):
            merged[k, s, 0, :, h * HS - base : (h + 1) * HS - base] = value.astype(jnp.bfloat16)

        def new_of(s, h):
            return arrived[k, s, 0, :, h * HS - base : (h + 1) * HS - base].astype(jnp.float32)

        into(k).wait()
        merge_head(old_ref, share, new_of, put, steps, width // HS, k)
        outof(k).start()
    for k in range(kv_heads):
        outof(k).wait()


def per_device(
    kv_weight, kv_bias, hidden_in, queries, res_cache, res_len, long_cache, long_len, long_dest
):
    step_count, _, serve_rows, width_part = hidden_in.shape
    kv_cols = kv_bias.shape[0]
    kv_heads = kv_cols // (2 * HS)
    query_cols = queries.shape[3]
    head_count = query_cols // HS
    per_kv = head_count // kv_heads
    staying = res_cache.shape[1]
    moving = serve_rows - staying
    rows = head_count * step_count
    tp_size = lax.axis_size("tp")
    tp_index = lax.axis_index("tp")
    group_index = lax.axis_index("grp")
    asked = lax.all_to_all(
        turn(queries, staying, kv_heads), "grp", split_axis=0, concat_axis=0, tiled=True
    )

    flat_hidden = hidden_in.reshape(step_count * serve_rows, width_part)
    pieces = project(flat_hidden, kv_weight, kv_cols, tp_size, tp_index, 1, tp_size - 1)
    others = jnp.stack(
        [
            lax.ppermute(pieces[j], "tp", [(i, (i + j + 1) % tp_size) for i in range(tp_size)])
            for j in range(tp_size - 1)
        ]
    )
    mine = project(flat_hidden, kv_weight, kv_cols, tp_size, tp_index, 0, 1)[0]

    answer = old_call(
        functools.partial(moving_kernel, kv_heads=kv_heads),
        [long_dest, long_len],
        asked,
        long_cache[0],
        rows,
        [
            pltpu.SMEM((moving + 8,), jnp.int32),
            pltpu.VMEM((moving, rows + STAT, HS), jnp.bfloat16),
            pltpu.SemaphoreType.DMA((moving,)),
            pltpu.SemaphoreType.DMA((moving,)),
        ],
        pltpu.HBM,
        48 * MIB,
        "moving_old",
    )
    answer, others, mine = lax.optimization_barrier((answer, others, mine))
    answer = lax.all_to_all(answer, "grp", split_axis=0, concat_axis=0, tiled=True)

    own_len = res_len[0]
    stayed = old_call(
        functools.partial(staying_kernel, kv_heads=kv_heads),
        [own_len],
        queries,
        res_cache[0],
        rows,
        [pltpu.VMEM((staying, rows, HS), jnp.bfloat16), pltpu.SemaphoreType.DMA((staying,))],
        pltpu.VMEM,
        58 * MIB,
        "staying_old",
    )
    matched = (long_dest == group_index).astype(jnp.int32)
    len_in = jnp.sum(matched * long_len, axis=1)
    served_len = jnp.concatenate([own_len, len_in])
    positions = served_len[None, :] + jnp.arange(step_count, dtype=jnp.int32)[:, None]
    half = HS // 2
    freqs = jnp.power(jnp.float32(ROPE_BASE), -2.0 * jnp.arange(half, dtype=jnp.float32) / HS)
    angles = positions.reshape(-1, 1).astype(jnp.float32) * freqs
    cosine, sine = jnp.cos(angles), jnp.sin(angles)
    cosine = jnp.concatenate([cosine, cosine], 1)
    sine = jnp.concatenate([-sine, sine], 1)

    out_shape = jax.ShapeDtypeStruct((step_count, 1, serve_rows, query_cols), jnp.bfloat16)
    fresh, lse = pl.pallas_call(
        functools.partial(new_kernel, kv_heads=kv_heads, per_kv=per_kv, staying=staying),
        out_shape=(out_shape, jax.ShapeDtypeStruct((serve_rows, HS), jnp.float32)),
        in_specs=[pl.BlockSpec(memory_space=pltpu.VMEM)] * 7,
        out_specs=(pl.BlockSpec(memory_space=pltpu.VMEM),) * 2,
        compiler_params=pltpu.CompilerParams(vmem_limit_bytes=24 * MIB),
        cost_estimate=pl.CostEstimate(
            flops=serve_rows * rows * step_count * serve_rows * HS * 4,
            bytes_accessed=8 * MIB,
            transcendentals=serve_rows * rows * step_count * serve_rows,
        ),
        name="new_part",
    )(queries, mine, others, kv_bias.reshape(1, kv_cols), cosine, sine, stayed)

    hbm, vmem = pl.BlockSpec(memory_space=pltpu.HBM), pl.BlockSpec(memory_space=pltpu.VMEM)
    part = (kv_heads, step_count, 1, moving, query_cols // kv_heads)
    return pl.pallas_call(
        functools.partial(join_kernel, kv_heads=kv_heads, first=staying),
        out_shape=out_shape,
        in_specs=[vmem, hbm, vmem],
        out_specs=hbm,
        scratch_shapes=[
            pltpu.VMEM(part, jnp.bfloat16),
            pltpu.VMEM(part, jnp.bfloat16),
            pltpu.SemaphoreType.DMA((kv_heads,)),
            pltpu.SemaphoreType.DMA((kv_heads,)),
        ],
        input_output_aliases={1: 0},
        compiler_params=pltpu.CompilerParams(vmem_limit_bytes=32 * MIB),
        cost_estimate=pl.CostEstimate(flops=MIB, bytes_accessed=2 * MIB, transcendentals=0),
        name="join",
    )(answer, fresh, lse)


def solution(mesh):
    placed = (
        P("tp", None),
        P("tp"),
        P(None, "grp", None, "tp"),
        P(None, "grp", None, "tp"),
        P("grp", None, None, "tp"),
        P("grp", None),
        P("grp", None, None, "tp"),
        P(),
        P(),
    )
    return jax.shard_map(
        per_device,
        mesh=mesh,
        in_specs=placed,
        out_specs=P(None, "grp", None, "tp"),
        check_vma=False,
    )
```

```python
import functools
import math

import jax
import jax.numpy as jnp
from jax import lax
from jax.experimental import pallas as pl
from jax.experimental.pallas import tpu as pltpu
from jax.sharding import PartitionSpec as P

HS = 128
ROPE_BASE = 1000000.0
masked_score = -1e30
SCALE = HS ** (-0.5)
LOG2E = math.log2(math.e)
STAT = 8
GROUP = 4
MIB = 1 << 20
FULL = 60 * MIB


def cache_copy(cache_ref, buf, sems, m, begin, end):
    part = pl.ds(begin, end - begin)
    sem = sems.at[0 if begin == 0 else 1, m]
    return pltpu.make_async_copy(cache_ref.at[m, part], buf.at[m, part], sem)


def moving_kernel(
    dest_hbm, length_hbm, query_ref, cache_ref, out_ref,
    buf, dest_ref, length_ref, order, answers, in_sems, out_sems, table_sems, *, kv_heads,
):
    count, capacity, _ = cache_ref.shape
    me = lax.axis_index("grp")
    chunk = min(capacity, 128)
    variants = capacity // chunk
    tables = [
        pltpu.make_async_copy(length_hbm, length_ref, table_sems.at[0]),
        pltpu.make_async_copy(dest_hbm, dest_ref, table_sems.at[1]),
    ]
    for table in tables:
        table.start()
    for m in range(count):
        cache_copy(cache_ref, buf, in_sems, m, 0, chunk).start()
    for table in tables:
        table.wait()
    used = [(length_ref[me, m] + chunk - 1) // chunk for m in range(count)]
    place = jnp.int32(0)
    for v in range(1, variants + 1):
        order[count + v] = place
        place = place + sum((u == v).astype(jnp.int32) for u in used)
    for m in range(count):
        at = order[count + used[m]]
        order[count + used[m]] = at + 1
        order[at] = m

    def leave(slot):
        return pltpu.make_async_copy(answers.at[slot], out_ref.at[slot], out_sems.at[slot])

    old_body(
        lambda m: dest_ref[me, m],
        lambda i: order[i],
        lambda m: length_ref[me, m],
        lambda slot, begin, end: query_ref[slot, begin:end, :],
        cache_ref, answers, buf, in_sems, kv_heads, lambda slot: leave(slot).start(),
    )

    @pl.loop(0, count)
    def _(slot):
        leave(slot).wait()


def staying_kernel(len_ref, query_ref, cache_ref, out_ref, buf, turned, sems, *, kv_heads):
    count, rows = out_ref.shape[0], out_ref.shape[1] - STAT

    steps, per = query_ref.shape[0], rows // kv_heads

    def same(m):
        return m

    for m in range(count):
        cache_copy(cache_ref, buf, sems, m, 0, min(cache_ref.shape[1], 128)).start()

    for k in range(kv_heads):
        turned[:, k * per : (k + 1) * per, :] = by_request(
            lambda s, q: query_ref[s, 0, 0:count, pl.ds((k * per // steps + q) * HS, HS)],
            steps, per // steps,
        )
    old_body(
        same, same, lambda m: len_ref[m], lambda m, begin, end: turned[m, begin:end, :],
        cache_ref, out_ref, buf, sems, kv_heads, lambda slot: None,
    )


def stat_rows(lses):
    rows = lses[0].shape[0]
    same = lax.broadcasted_iota(jnp.int32, (rows, HS), 0) == lax.broadcasted_iota(
        jnp.int32, (rows, HS), 1
    )
    row = lax.broadcasted_iota(jnp.int32, (STAT, HS), 0)
    result = []
    for lse in lses:
        turned = jnp.sum(jnp.where(same, lse, 0.0), axis=0, keepdims=True)
        whole = jnp.broadcast_to(turned, (STAT, HS))
        high = whole.astype(jnp.bfloat16).astype(jnp.float32)
        rest = whole - high
        middle = rest.astype(jnp.bfloat16).astype(jnp.float32)
        terms = jnp.where(row == 0, high, jnp.where(row == 1, middle, rest - middle))
        result.append(jnp.where(row < 3, terms, 0.0).astype(jnp.bfloat16))
    return result


def old_body(slot_of, member, length_of, query_of, cache_ref, out_ref, buf, sems, kv_heads, done):
    count, capacity, _ = cache_ref.shape
    rows = out_ref.shape[1] - STAT
    per = rows // kv_heads
    chunk = min(capacity, 128)
    variants = capacity // chunk
    pair = 2 if kv_heads % 2 == 0 else 1

    def run(act):
        @pl.loop(0, count // GROUP)
        def _(g):
            members = [member(g * GROUP + i) for i in range(GROUP)]
            if variants == 1:
                act(members, 1)
                return
            used = (length_of(members[-1]) + chunk - 1) // chunk
            for v in range(1, variants + 1):
                pl.when(used == v)(functools.partial(act, members, v))

    def start(members, v):
        if v > 1:
            for m in members:
                cache_copy(cache_ref, buf, sems, m, chunk, v * chunk).start()

    def body(members, v):
        size, length = len(members), v * chunk
        for m in members:
            cache_copy(cache_ref, buf, sems, m, 0, chunk).wait()
            if v > 1:
                cache_copy(cache_ref, buf, sems, m, chunk, length).wait()
        slots = [slot_of(m) for m in members]
        column = lax.broadcasted_iota(jnp.int32, (pair * per, length), 1)
        part = pl.ds(0, length)
        items = [
            (i, [p * pair + j for j in range(pair)])
            for i in range(size)
            for p in range(kv_heads // pair)
        ]
        queries = []
        for i, heads in items:
            own = [query_of(slots[i], h * per, (h + 1) * per) for h in heads]
            if pair == 2:
                zero = jnp.zeros_like(own[0])
                own = [
                    jnp.concatenate(
                        [jnp.concatenate([own[0], zero], 1), jnp.concatenate([zero, own[1]], 1)], 0
                    )
                ]
            queries.append(own[0])

        def columns(i, heads, shift):
            at = [h * 2 * HS + shift for h in heads]
            return jnp.concatenate([buf[members[i], part, c : c + HS] for c in at], 1)

        scores = [
            lax.dot_general(
                query, columns(i, heads, 0), (((1,), (1,)), ((), ())),
                preferred_element_type=jnp.float32,
            )
            for query, (i, heads) in zip(queries, items)
        ]
        scores = [
            jnp.where(column < length_of(members[i]), x, masked_score)
            for x, (i, _) in zip(scores, items)
        ]
        highest = [jnp.max(x, axis=1, keepdims=True) for x in scores]
        probs = [jnp.exp2((x - h) * (SCALE * LOG2E)) for x, h in zip(scores, highest)]
        total = [jnp.sum(x, axis=1, keepdims=True) for x in probs]
        probs = [x.astype(jnp.bfloat16) for x in probs]
        mixed = [
            jnp.dot(x, columns(i, heads, HS), preferred_element_type=jnp.float32)
            for x, (i, heads) in zip(probs, items)
        ]
        mixed = [x * (1.0 / t) for x, t in zip(mixed, total)]
        lses = [h * SCALE + jnp.log(t) for h, t in zip(highest, total)]
        terms = stat_rows(
            [
                jnp.concatenate([x for x, (o, _) in zip(lses, items) if o == i], 0)
                for i in range(size)
            ]
        )
        for x, (i, heads) in zip(mixed, items):
            for j, h in enumerate(heads):
                out_ref[slots[i], h * per : (h + 1) * per, :] = x[
                    j * per : (j + 1) * per, j * HS : (j + 1) * HS
                ].astype(jnp.bfloat16)
        for i in range(size):
            out_ref[slots[i], rows : rows + STAT, :] = terms[i]
            done(slots[i])

    if variants > 1:
        run(start)
    run(body)


def by_request(tile_of, steps, per_kv):
    tiles = [tile_of(s, q) for s in range(steps) for q in range(per_kv)]
    return jnp.swapaxes(jnp.stack(tiles, 0), 0, 1)


def turn_kernel(query_ref, out_ref, arrived, turned, in_sems, out_sems, *, kv_heads, first):
    count, rows, _ = out_ref.shape
    steps = query_ref.shape[0]
    per = rows // kv_heads
    width = query_ref.shape[3] // kv_heads
    own = pl.ds(first, count)

    def into(k):
        lanes = pl.ds(k * width, width)
        return pltpu.make_async_copy(
            query_ref.at[:, :, own, lanes], arrived.at[k], in_sems.at[k]
        )

    def outof(k):
        return pltpu.make_async_copy(
            turned.at[k], out_ref.at[:, pl.ds(k * per, per), :], out_sems.at[k]
        )

    for k in range(kv_heads):
        into(k).start()
    for k in range(kv_heads):
        into(k).wait()
        turned[k] = by_request(
            lambda s, q: arrived[k, s, 0, :, q * HS : (q + 1) * HS], steps, per // steps
        )
        outof(k).start()
    for k in range(kv_heads):
        outof(k).wait()


def turn(queries, first, kv_heads):
    steps, _, serve, cols = queries.shape
    count, width = serve - first, cols // kv_heads
    per = steps * width // HS
    return pl.pallas_call(
        functools.partial(turn_kernel, kv_heads=kv_heads, first=first),
        out_shape=jax.ShapeDtypeStruct((count, kv_heads * per, HS), jnp.bfloat16),
        in_specs=[pl.BlockSpec(memory_space=pltpu.HBM)],
        out_specs=pl.BlockSpec(memory_space=pltpu.HBM),
        scratch_shapes=[
            pltpu.VMEM((kv_heads, steps, 1, count, width), jnp.bfloat16),
            pltpu.VMEM((kv_heads, count, per, HS), jnp.bfloat16),
            pltpu.SemaphoreType.DMA((kv_heads,)),
            pltpu.SemaphoreType.DMA((kv_heads,)),
        ],
        compiler_params=pltpu.CompilerParams(vmem_limit_bytes=FULL),
        cost_estimate=pl.CostEstimate(flops=MIB, bytes_accessed=MIB, transcendentals=0),
        name="turn",
    )(queries)


def project_kernel(index_ref, hidden_ref, weight_ref, out_ref):
    del index_ref
    out_ref[0] = jnp.dot(hidden_ref[...], weight_ref[...], preferred_element_type=jnp.float32)


def project(hidden, weight, kv_cols, tp_size, tp_index, first, pieces):
    rows, depth = hidden.shape
    width = min(kv_cols, 256)
    blocks = kv_cols // width
    return pl.pallas_call(
        project_kernel,
        out_shape=jax.ShapeDtypeStruct((pieces, rows, kv_cols), jnp.float32),
        grid_spec=pltpu.PrefetchScalarGridSpec(
            num_scalar_prefetch=1,
            grid=(pieces, blocks),
            in_specs=[
                pl.BlockSpec((rows, depth), lambda j, c, index: (0, 0)),
                pl.BlockSpec(
                    (depth, width),
                    lambda j, c, index: (0, lax.rem(index[0] + first + j, tp_size) * blocks + c),
                ),
            ],
            out_specs=pl.BlockSpec((1, rows, width), lambda j, c, index: (j, 0, c)),
        ),
        compiler_params=pltpu.CompilerParams(vmem_limit_bytes=FULL),
        cost_estimate=pl.CostEstimate(
            flops=2 * rows * depth * kv_cols * pieces,
            bytes_accessed=depth * kv_cols * pieces * 2,
            transcendentals=0,
        ),
        name="project",
    )(tp_index.reshape(1), hidden, weight)


def old_call(kernel, scalars, scalar_space, query, cache, rows, scratch, out_space, limit, name):
    count, capacity, _ = cache.shape
    scalar, vmem = pl.BlockSpec(memory_space=scalar_space), pl.BlockSpec(memory_space=pltpu.VMEM)
    return pl.pallas_call(
        kernel,
        out_shape=jax.ShapeDtypeStruct((count, rows + STAT, HS), jnp.bfloat16),
        in_specs=[scalar] * len(scalars) + [vmem, pl.BlockSpec(memory_space=pltpu.HBM)],
        out_specs=pl.BlockSpec(memory_space=out_space),
        scratch_shapes=[pltpu.VMEM(cache.shape, jnp.bfloat16)] + scratch,
        compiler_params=pltpu.CompilerParams(vmem_limit_bytes=limit),
        cost_estimate=pl.CostEstimate(
            flops=count * rows * capacity * HS * 8,
            bytes_accessed=cache.size * 2,
            transcendentals=count * rows * capacity,
        ),
        name=name,
    )(*scalars, query, cache)


def old_lse(stat):
    return stat[:, 0, :] + stat[:, 1, :] + stat[:, 2, :]


def merge_head(old_ref, share, put, steps, per_kv, k):
    per = steps * per_kv
    old = jnp.swapaxes(old_ref[:, k * per : (k + 1) * per, :], 0, 1).astype(jnp.float32)
    for s in range(steps):
        for q in range(per_kv):
            at = s * per_kv + q
            c = k * per + at
            put(s, k * per_kv + q, share[:, c : c + 1] * old[at], share[:, c : c + 1])


def new_kernel(
    query_ref, mine_ref, other_ref, bias_ref, cos_ref, sin_ref, old_ref, out_ref, lse_ref,
    *, kv_heads, per_kv, staying,
):
    steps, _, serve, _ = query_ref.shape
    rows = old_ref.shape[1] - STAT
    raw = mine_ref[...]
    for i in range(other_ref.shape[0]):
        raw = raw + other_ref[i]
    raw = raw + bias_ref[...].astype(jnp.float32)
    total_rows = steps * serve
    request = lax.broadcasted_iota(jnp.int32, (serve, total_rows), 0)
    column = lax.broadcasted_iota(jnp.int32, (serve, total_rows), 1)
    lane = lax.broadcasted_iota(jnp.int32, (serve, HS), 1)
    lse_all = jnp.zeros((serve, HS), jnp.float32)
    for k in range(kv_heads):
        keys = raw[:, k * 2 * HS : k * 2 * HS + HS]
        keys = keys * cos_ref[...] + pltpu.roll(keys, HS // 2, 1) * sin_ref[...]
        keys = keys.astype(jnp.bfloat16)
        values = raw[:, k * 2 * HS + HS : (k + 1) * 2 * HS].astype(jnp.bfloat16)
        for s in range(steps):
            heads = [k * per_kv + q for q in range(per_kv)]
            query = jnp.concatenate([query_ref[s, 0, :, h * HS : (h + 1) * HS] for h in heads], 0)
            scores = lax.dot_general(
                query, keys, (((1,), (1,)), ((), ())), preferred_element_type=jnp.float32
            )
            seen = column == request
            for t in range(1, s + 1):
                seen = seen | (column == request + t * serve)
            scores = jnp.where(jnp.concatenate([seen] * per_kv, 0), scores, masked_score)
            highest = jnp.max(scores, axis=1, keepdims=True)
            probs = jnp.exp2((scores - highest) * (SCALE * LOG2E))
            total = jnp.sum(probs, axis=1, keepdims=True)
            mixed = jnp.dot(probs.astype(jnp.bfloat16), values, preferred_element_type=jnp.float32)
            mixed = mixed * (1.0 / total)
            lse = highest * SCALE + jnp.log(total)
            for q, h in enumerate(heads):
                c = (k * steps + s) * per_kv + q
                lse_all = jnp.where(lane == c, lse[q * serve : (q + 1) * serve], lse_all)
                out_ref[s, 0, :, h * HS : (h + 1) * HS] = mixed[
                    q * serve : (q + 1) * serve
                ].astype(jnp.bfloat16)
    lse_ref[...] = lse_all

    def put(s, h, old, weight):
        lanes = pl.ds(h * HS, HS)
        new = out_ref[s, 0, 0:staying, lanes].astype(jnp.float32)
        out_ref[s, 0, 0:staying, lanes] = (old + (1.0 - weight) * new).astype(jnp.bfloat16)

    stat = old_lse(old_ref[:, rows : rows + STAT, :].astype(jnp.float32))
    share = 1.0 / (1.0 + jnp.exp(lse_all[0:staying] - stat))
    for k in range(kv_heads):
        merge_head(old_ref, share, put, steps, per_kv, k)


def join_kernel(
    old_ref, new_ref, lse_ref, out_ref, arrived, weighted, weights, merged, in_sems, out_sems,
    *, kv_heads, first,
):
    steps = new_ref.shape[0]
    count, rows = old_ref.shape[0], old_ref.shape[1] - STAT
    width = new_ref.shape[3] // kv_heads
    per_kv = width // HS
    own = pl.ds(first, count)

    def into(k):
        lanes = pl.ds(k * width, width)
        return pltpu.make_async_copy(new_ref.at[:, :, own, lanes], arrived.at[k], in_sems.at[k])

    def outof(k):
        lanes = pl.ds(k * width, width)
        return pltpu.make_async_copy(merged.at[k], out_ref.at[:, :, own, lanes], out_sems.at[k])

    for k in range(kv_heads):
        into(k).start()
    stat = old_lse(old_ref[:, rows : rows + STAT, :].astype(jnp.float32))
    share = 1.0 / (1.0 + jnp.exp(lse_ref[first : first + count, :] - stat))

    def put(s, h, old, weight):
        weighted[s, h] = old
        weights[s, h] = jnp.broadcast_to(1.0 - weight, (count, HS))

    for k in range(kv_heads):
        merge_head(old_ref, share, put, steps, per_kv, k)
    for k in range(kv_heads):
        into(k).wait()
        for s in range(steps):
            for q in range(per_kv):
                h, lanes = k * per_kv + q, pl.ds(q * HS, HS)
                new = arrived[k, s, 0, :, lanes].astype(jnp.float32)
                merged[k, s, 0, :, lanes] = (weighted[s, h] + weights[s, h] * new).astype(
                    jnp.bfloat16
                )
        outof(k).start()
    for k in range(kv_heads):
        outof(k).wait()


def per_device(
    kv_weight, kv_bias, hidden_in, queries, res_cache, res_len, long_cache, long_len, long_dest
):
    step_count, _, serve_rows, width_part = hidden_in.shape
    kv_cols = kv_bias.shape[0]
    kv_heads = kv_cols // (2 * HS)
    query_cols = queries.shape[3]
    head_count = query_cols // HS
    per_kv = head_count // kv_heads
    staying = res_cache.shape[1]
    moving = serve_rows - staying
    rows = head_count * step_count
    tp_size = lax.axis_size("tp")
    tp_index = lax.axis_index("tp")
    group_index = lax.axis_index("grp")
    asked = lax.all_to_all(
        turn(queries, staying, kv_heads), "grp", split_axis=0, concat_axis=0, tiled=True
    )

    flat_hidden = hidden_in.reshape(step_count * serve_rows, width_part)
    pieces = project(flat_hidden, kv_weight, kv_cols, tp_size, tp_index, 1, tp_size - 1)
    others = jnp.stack(
        [
            lax.ppermute(pieces[j], "tp", [(i, (i + j + 1) % tp_size) for i in range(tp_size)])
            for j in range(tp_size - 1)
        ]
    )
    mine = project(flat_hidden, kv_weight, kv_cols, tp_size, tp_index, 0, 1)[0]

    answer = old_call(
        functools.partial(moving_kernel, kv_heads=kv_heads),
        [long_dest, long_len],
        pltpu.HBM,
        asked,
        long_cache[0],
        rows,
        [
            pltpu.SMEM(long_dest.shape, jnp.int32),
            pltpu.SMEM(long_len.shape, jnp.int32),
            pltpu.SMEM((moving + 8,), jnp.int32),
            pltpu.VMEM((moving, rows + STAT, HS), jnp.bfloat16),
            pltpu.SemaphoreType.DMA((2, moving)),
            pltpu.SemaphoreType.DMA((moving,)),
            pltpu.SemaphoreType.DMA((2,)),
        ],
        pltpu.HBM,
        48 * MIB,
        "moving_old",
    )
    answer, others, mine = lax.optimization_barrier((answer, others, mine))
    answer = lax.all_to_all(answer, "grp", split_axis=0, concat_axis=0, tiled=True)

    own_len = res_len[0]
    stayed = old_call(
        functools.partial(staying_kernel, kv_heads=kv_heads),
        [own_len],
        pltpu.SMEM,
        queries,
        res_cache[0],
        rows,
        [pltpu.VMEM((staying, rows, HS), jnp.bfloat16), pltpu.SemaphoreType.DMA((2, staying))],
        pltpu.VMEM,
        58 * MIB,
        "staying_old",
    )
    matched = (long_dest == group_index).astype(jnp.int32)
    len_in = jnp.sum(matched * long_len, axis=1)
    served_len = jnp.concatenate([own_len, len_in])
    positions = served_len[None, :] + jnp.arange(step_count, dtype=jnp.int32)[:, None]
    half = HS // 2
    freqs = jnp.power(jnp.float32(ROPE_BASE), -2.0 * jnp.arange(half, dtype=jnp.float32) / HS)
    angles = positions.reshape(-1, 1).astype(jnp.float32) * freqs
    cosine, sine = jnp.cos(angles), jnp.sin(angles)
    cosine = jnp.concatenate([cosine, cosine], 1)
    sine = jnp.concatenate([-sine, sine], 1)

    out_shape = jax.ShapeDtypeStruct((step_count, 1, serve_rows, query_cols), jnp.bfloat16)
    fresh, lse = pl.pallas_call(
        functools.partial(new_kernel, kv_heads=kv_heads, per_kv=per_kv, staying=staying),
        out_shape=(out_shape, jax.ShapeDtypeStruct((serve_rows, HS), jnp.float32)),
        in_specs=[pl.BlockSpec(memory_space=pltpu.VMEM)] * 7,
        out_specs=(pl.BlockSpec(memory_space=pltpu.VMEM),) * 2,
        compiler_params=pltpu.CompilerParams(vmem_limit_bytes=24 * MIB),
        cost_estimate=pl.CostEstimate(
            flops=serve_rows * rows * step_count * serve_rows * HS * 4,
            bytes_accessed=8 * MIB,
            transcendentals=serve_rows * rows * step_count * serve_rows,
        ),
        name="new_part",
    )(queries, mine, others, kv_bias.reshape(1, kv_cols), cosine, sine, stayed)

    hbm, vmem = pl.BlockSpec(memory_space=pltpu.HBM), pl.BlockSpec(memory_space=pltpu.VMEM)
    part = (kv_heads, step_count, 1, moving, query_cols // kv_heads)
    return pl.pallas_call(
        functools.partial(join_kernel, kv_heads=kv_heads, first=staying),
        out_shape=out_shape,
        in_specs=[vmem, hbm, vmem],
        out_specs=hbm,
        scratch_shapes=[
            pltpu.VMEM(part, jnp.bfloat16),
            pltpu.VMEM((step_count, head_count, moving, HS), jnp.float32),
            pltpu.VMEM((step_count, head_count, moving, HS), jnp.float32),
            pltpu.VMEM(part, jnp.bfloat16),
            pltpu.SemaphoreType.DMA((kv_heads,)),
            pltpu.SemaphoreType.DMA((kv_heads,)),
        ],
        input_output_aliases={1: 0},
        compiler_params=pltpu.CompilerParams(vmem_limit_bytes=32 * MIB),
        cost_estimate=pl.CostEstimate(flops=MIB, bytes_accessed=2 * MIB, transcendentals=0),
        name="join",
    )(answer, fresh, lse)


def solution(mesh):
    placed = (
        P("tp", None),
        P("tp"),
        P(None, "grp", None, "tp"),
        P(None, "grp", None, "tp"),
        P("grp", None, None, "tp"),
        P("grp", None),
        P("grp", None, None, "tp"),
        P(),
        P(),
    )
    return jax.shard_map(
        per_device,
        mesh=mesh,
        in_specs=placed,
        out_specs=P(None, "grp", None, "tp"),
        check_vma=False,
    )
```

```python
import functools
import math

import jax
import jax.numpy as jnp
from jax import lax
from jax.experimental import pallas as pl
from jax.experimental.pallas import tpu as pltpu
from jax.sharding import PartitionSpec as P

HS = 128
ROPE_BASE = 1000000.0
masked_score = -1e30
SCALE = HS ** (-0.5)
LOG2E = math.log2(math.e)
STAT = 8
GROUP = 4
MIB = 1 << 20
FULL = 60 * MIB


def cache_copy(cache_ref, buf, sems, m, begin, end):
    part = pl.ds(begin, end - begin)
    sem = sems.at[0 if begin == 0 else 1, m]
    return pltpu.make_async_copy(cache_ref.at[m, part], buf.at[m, part], sem)


def moving_kernel(
    dest_hbm, length_hbm, query_ref, cache_ref, out_ref,
    buf, dest_ref, length_ref, order, answers, in_sems, out_sems, table_sems, *, kv_heads,
):
    count, capacity, _ = cache_ref.shape
    me = lax.axis_index("grp")
    chunk = min(capacity, 128)
    variants = capacity // chunk
    tables = [
        pltpu.make_async_copy(length_hbm, length_ref, table_sems.at[0]),
        pltpu.make_async_copy(dest_hbm, dest_ref, table_sems.at[1]),
    ]
    for table in tables:
        table.start()
    for m in range(count):
        cache_copy(cache_ref, buf, in_sems, m, 0, chunk).start()
    for table in tables:
        table.wait()
    used = [(length_ref[me, m] + chunk - 1) // chunk for m in range(count)]
    place = jnp.int32(0)
    for v in range(1, variants + 1):
        order[count + v] = place
        place = place + sum((u == v).astype(jnp.int32) for u in used)
    for m in range(count):
        at = order[count + used[m]]
        order[count + used[m]] = at + 1
        order[at] = m

    def leave(slot):
        return pltpu.make_async_copy(answers.at[slot], out_ref.at[slot], out_sems.at[slot])

    old_body(
        lambda m: dest_ref[me, m],
        lambda i: order[i],
        lambda m: length_ref[me, m],
        lambda slot, begin, end: query_ref[slot, begin:end, :],
        cache_ref, answers, buf, in_sems, kv_heads, lambda slot: leave(slot).start(),
    )

    @pl.loop(0, count)
    def _(slot):
        leave(slot).wait()


def staying_kernel(len_ref, query_ref, cache_ref, out_ref, buf, turned, sems, *, kv_heads):
    count, rows = out_ref.shape[0], out_ref.shape[1] - STAT

    steps, per = query_ref.shape[0], rows // kv_heads

    def same(m):
        return m

    for m in range(count):
        cache_copy(cache_ref, buf, sems, m, 0, min(cache_ref.shape[1], 128)).start()

    for k in range(kv_heads):
        turned[:, k * per : (k + 1) * per, :] = by_request(
            lambda s, q: query_ref[s, 0, 0:count, pl.ds((k * per // steps + q) * HS, HS)],
            steps, per // steps,
        )
    old_body(
        same, same, lambda m: len_ref[m], lambda m, begin, end: turned[m, begin:end, :],
        cache_ref, out_ref, buf, sems, kv_heads, lambda slot: None,
    )


def stat_rows(lses):
    rows = lses[0].shape[0]
    same = lax.broadcasted_iota(jnp.int32, (rows, HS), 0) == lax.broadcasted_iota(
        jnp.int32, (rows, HS), 1
    )
    row = lax.broadcasted_iota(jnp.int32, (STAT, HS), 0)
    result = []
    for lse in lses:
        turned = jnp.sum(jnp.where(same, lse, 0.0), axis=0, keepdims=True)
        whole = jnp.broadcast_to(turned, (STAT, HS))
        high = whole.astype(jnp.bfloat16).astype(jnp.float32)
        rest = whole - high
        middle = rest.astype(jnp.bfloat16).astype(jnp.float32)
        terms = jnp.where(row == 0, high, jnp.where(row == 1, middle, rest - middle))
        result.append(jnp.where(row < 3, terms, 0.0).astype(jnp.bfloat16))
    return result


def old_body(slot_of, member, length_of, query_of, cache_ref, out_ref, buf, sems, kv_heads, done):
    count, capacity, _ = cache_ref.shape
    rows = out_ref.shape[1] - STAT
    per = rows // kv_heads
    chunk = min(capacity, 128)
    variants = capacity // chunk
    pair = 2 if kv_heads % 2 == 0 else 1

    def run(act):
        @pl.loop(0, count // GROUP)
        def _(g):
            members = [member(g * GROUP + i) for i in range(GROUP)]
            if variants == 1:
                act(members, 1)
                return
            used = (length_of(members[-1]) + chunk - 1) // chunk
            for v in range(1, variants + 1):
                pl.when(used == v)(functools.partial(act, members, v))

    def start(members, v):
        if v > 1:
            for m in members:
                cache_copy(cache_ref, buf, sems, m, chunk, v * chunk).start()

    def body(members, v):
        size, length = len(members), v * chunk
        for m in members:
            cache_copy(cache_ref, buf, sems, m, 0, chunk).wait()
            if v > 1:
                cache_copy(cache_ref, buf, sems, m, chunk, length).wait()
        slots = [slot_of(m) for m in members]
        column = lax.broadcasted_iota(jnp.int32, (pair * per, length), 1)
        part = pl.ds(0, length)
        items = [
            (i, [p * pair + j for j in range(pair)])
            for i in range(size)
            for p in range(kv_heads // pair)
        ]
        queries = []
        for i, heads in items:
            own = [query_of(slots[i], h * per, (h + 1) * per) for h in heads]
            if pair == 2:
                zero = jnp.zeros_like(own[0])
                own = [
                    jnp.concatenate(
                        [jnp.concatenate([own[0], zero], 1), jnp.concatenate([zero, own[1]], 1)], 0
                    )
                ]
            queries.append(own[0])

        def columns(i, heads, shift):
            at = [h * 2 * HS + shift for h in heads]
            return jnp.concatenate([buf[members[i], part, c : c + HS] for c in at], 1)

        scores = [
            lax.dot_general(
                query, columns(i, heads, 0), (((1,), (1,)), ((), ())),
                preferred_element_type=jnp.float32,
            )
            for query, (i, heads) in zip(queries, items)
        ]
        scores = [
            jnp.where(column < length_of(members[i]), x, masked_score)
            for x, (i, _) in zip(scores, items)
        ]
        highest = [jnp.max(x, axis=1, keepdims=True) for x in scores]
        probs = [jnp.exp2((x - h) * (SCALE * LOG2E)) for x, h in zip(scores, highest)]
        total = [jnp.sum(x, axis=1, keepdims=True) for x in probs]
        probs = [x.astype(jnp.bfloat16) for x in probs]
        mixed = [
            jnp.dot(x, columns(i, heads, HS), preferred_element_type=jnp.float32)
            for x, (i, heads) in zip(probs, items)
        ]
        mixed = [x * (1.0 / t) for x, t in zip(mixed, total)]
        lses = [h * SCALE + jnp.log(t) for h, t in zip(highest, total)]
        terms = stat_rows(
            [
                jnp.concatenate([x for x, (o, _) in zip(lses, items) if o == i], 0)
                for i in range(size)
            ]
        )
        for x, (i, heads) in zip(mixed, items):
            for j, h in enumerate(heads):
                out_ref[slots[i], h * per : (h + 1) * per, :] = x[
                    j * per : (j + 1) * per, j * HS : (j + 1) * HS
                ].astype(jnp.bfloat16)
        for i in range(size):
            out_ref[slots[i], rows : rows + STAT, :] = terms[i]
            done(slots[i])

    if variants > 1:
        run(start)
    run(body)


def by_request(tile_of, steps, per_kv):
    tiles = [tile_of(s, q) for s in range(steps) for q in range(per_kv)]
    return jnp.swapaxes(jnp.stack(tiles, 0), 0, 1)


def turn_kernel(query_ref, out_ref, arrived, turned, in_sems, out_sems, *, kv_heads, first):
    count, rows, _ = out_ref.shape
    steps = query_ref.shape[0]
    per = rows // kv_heads
    width = query_ref.shape[3] // kv_heads
    own = pl.ds(first, count)

    def into(k):
        lanes = pl.ds(k * width, width)
        return pltpu.make_async_copy(
            query_ref.at[:, :, own, lanes], arrived.at[k], in_sems.at[k]
        )

    def outof(k):
        return pltpu.make_async_copy(
            turned.at[k], out_ref.at[:, pl.ds(k * per, per), :], out_sems.at[k]
        )

    for k in range(kv_heads):
        into(k).start()
    for k in range(kv_heads):
        into(k).wait()
        turned[k] = by_request(
            lambda s, q: arrived[k, s, 0, :, q * HS : (q + 1) * HS], steps, per // steps
        )
        outof(k).start()
    for k in range(kv_heads):
        outof(k).wait()


def turn(queries, first, kv_heads):
    steps, _, serve, cols = queries.shape
    count, width = serve - first, cols // kv_heads
    per = steps * width // HS
    return pl.pallas_call(
        functools.partial(turn_kernel, kv_heads=kv_heads, first=first),
        out_shape=jax.ShapeDtypeStruct((count, kv_heads * per, HS), jnp.bfloat16),
        in_specs=[pl.BlockSpec(memory_space=pltpu.HBM)],
        out_specs=pl.BlockSpec(memory_space=pltpu.HBM),
        scratch_shapes=[
            pltpu.VMEM((kv_heads, steps, 1, count, width), jnp.bfloat16),
            pltpu.VMEM((kv_heads, count, per, HS), jnp.bfloat16),
            pltpu.SemaphoreType.DMA((kv_heads,)),
            pltpu.SemaphoreType.DMA((kv_heads,)),
        ],
        compiler_params=pltpu.CompilerParams(vmem_limit_bytes=FULL),
        cost_estimate=pl.CostEstimate(flops=MIB, bytes_accessed=MIB, transcendentals=0),
        name="turn",
    )(queries)


def project_kernel(index_ref, hidden_ref, weight_ref, out_ref):
    del index_ref
    out_ref[0] = jnp.dot(hidden_ref[...], weight_ref[...], preferred_element_type=jnp.float32)


def project(hidden, weight, kv_cols, tp_size, tp_index, first, pieces):
    rows, depth = hidden.shape
    width = min(kv_cols, 512)
    blocks = kv_cols // width
    return pl.pallas_call(
        project_kernel,
        out_shape=jax.ShapeDtypeStruct((pieces, rows, kv_cols), jnp.float32),
        grid_spec=pltpu.PrefetchScalarGridSpec(
            num_scalar_prefetch=1,
            grid=(pieces, blocks),
            in_specs=[
                pl.BlockSpec((rows, depth), lambda j, c, index: (0, 0)),
                pl.BlockSpec(
                    (depth, width),
                    lambda j, c, index: (0, lax.rem(index[0] + first + j, tp_size) * blocks + c),
                ),
            ],
            out_specs=pl.BlockSpec((1, rows, width), lambda j, c, index: (j, 0, c)),
        ),
        compiler_params=pltpu.CompilerParams(vmem_limit_bytes=FULL),
        cost_estimate=pl.CostEstimate(
            flops=2 * rows * depth * kv_cols * pieces,
            bytes_accessed=depth * kv_cols * pieces * 2,
            transcendentals=0,
        ),
        name="project",
    )(tp_index.reshape(1), hidden, weight)


def old_call(kernel, scalars, scalar_space, query, cache, rows, scratch, out_space, limit, name):
    count, capacity, _ = cache.shape
    scalar, vmem = pl.BlockSpec(memory_space=scalar_space), pl.BlockSpec(memory_space=pltpu.VMEM)
    return pl.pallas_call(
        kernel,
        out_shape=jax.ShapeDtypeStruct((count, rows + STAT, HS), jnp.bfloat16),
        in_specs=[scalar] * len(scalars) + [vmem, pl.BlockSpec(memory_space=pltpu.HBM)],
        out_specs=pl.BlockSpec(memory_space=out_space),
        scratch_shapes=[pltpu.VMEM(cache.shape, jnp.bfloat16)] + scratch,
        compiler_params=pltpu.CompilerParams(vmem_limit_bytes=limit),
        cost_estimate=pl.CostEstimate(
            flops=count * rows * capacity * HS * 8,
            bytes_accessed=cache.size * 2,
            transcendentals=count * rows * capacity,
        ),
        name=name,
    )(*scalars, query, cache)


def old_lse(stat):
    return stat[:, 0, :] + stat[:, 1, :] + stat[:, 2, :]


def merge_head(old_ref, share, put, steps, per_kv, k):
    per = steps * per_kv
    old = jnp.swapaxes(old_ref[:, k * per : (k + 1) * per, :], 0, 1).astype(jnp.float32)
    for s in range(steps):
        for q in range(per_kv):
            at = s * per_kv + q
            c = k * per + at
            put(s, k * per_kv + q, share[:, c : c + 1] * old[at], share[:, c : c + 1])


def new_kernel(
    query_ref, mine_ref, other_ref, bias_ref, cos_ref, sin_ref, old_ref, out_ref, lse_ref,
    *, kv_heads, per_kv, staying,
):
    steps, _, serve, _ = query_ref.shape
    rows = old_ref.shape[1] - STAT
    raw = mine_ref[...]
    for i in range(other_ref.shape[0]):
        raw = raw + other_ref[i]
    raw = raw + bias_ref[...].astype(jnp.float32)
    total_rows = steps * serve
    request = lax.broadcasted_iota(jnp.int32, (serve, total_rows), 0)
    column = lax.broadcasted_iota(jnp.int32, (serve, total_rows), 1)
    lane = lax.broadcasted_iota(jnp.int32, (serve, HS), 1)
    lse_all = jnp.zeros((serve, HS), jnp.float32)
    for k in range(kv_heads):
        keys = raw[:, k * 2 * HS : k * 2 * HS + HS]
        keys = keys * cos_ref[...] + pltpu.roll(keys, HS // 2, 1) * sin_ref[...]
        keys = keys.astype(jnp.bfloat16)
        values = raw[:, k * 2 * HS + HS : (k + 1) * 2 * HS].astype(jnp.bfloat16)
        for s in range(steps):
            heads = [k * per_kv + q for q in range(per_kv)]
            query = jnp.concatenate([query_ref[s, 0, :, h * HS : (h + 1) * HS] for h in heads], 0)
            scores = lax.dot_general(
                query, keys, (((1,), (1,)), ((), ())), preferred_element_type=jnp.float32
            )
            seen = column == request
            for t in range(1, s + 1):
                seen = seen | (column == request + t * serve)
            scores = jnp.where(jnp.concatenate([seen] * per_kv, 0), scores, masked_score)
            highest = jnp.max(scores, axis=1, keepdims=True)
            probs = jnp.exp2((scores - highest) * (SCALE * LOG2E))
            total = jnp.sum(probs, axis=1, keepdims=True)
            mixed = jnp.dot(probs.astype(jnp.bfloat16), values, preferred_element_type=jnp.float32)
            mixed = mixed * (1.0 / total)
            lse = highest * SCALE + jnp.log(total)
            for q, h in enumerate(heads):
                c = (k * steps + s) * per_kv + q
                lse_all = jnp.where(lane == c, lse[q * serve : (q + 1) * serve], lse_all)
                out_ref[s, 0, :, h * HS : (h + 1) * HS] = mixed[
                    q * serve : (q + 1) * serve
                ].astype(jnp.bfloat16)
    lse_ref[...] = lse_all

    def put(s, h, old, weight):
        lanes = pl.ds(h * HS, HS)
        new = out_ref[s, 0, 0:staying, lanes].astype(jnp.float32)
        out_ref[s, 0, 0:staying, lanes] = (old + (1.0 - weight) * new).astype(jnp.bfloat16)

    stat = old_lse(old_ref[:, rows : rows + STAT, :].astype(jnp.float32))
    share = 1.0 / (1.0 + jnp.exp(lse_all[0:staying] - stat))
    for k in range(kv_heads):
        merge_head(old_ref, share, put, steps, per_kv, k)


def join_kernel(
    old_ref, new_ref, lse_ref, out_ref, arrived, weighted, weights, merged, in_sems, out_sems,
    *, kv_heads, first,
):
    steps = new_ref.shape[0]
    count, rows = old_ref.shape[0], old_ref.shape[1] - STAT
    width = new_ref.shape[3] // kv_heads
    per_kv = width // HS
    own = pl.ds(first, count)

    def into(k):
        lanes = pl.ds(k * width, width)
        return pltpu.make_async_copy(new_ref.at[:, :, own, lanes], arrived.at[k], in_sems.at[k])

    def outof(k):
        lanes = pl.ds(k * width, width)
        return pltpu.make_async_copy(merged.at[k], out_ref.at[:, :, own, lanes], out_sems.at[k])

    for k in range(kv_heads):
        into(k).start()
    stat = old_lse(old_ref[:, rows : rows + STAT, :].astype(jnp.float32))
    share = 1.0 / (1.0 + jnp.exp(lse_ref[first : first + count, :] - stat))

    def put(s, h, old, weight):
        weighted[s, h] = old
        weights[s, h] = jnp.broadcast_to(1.0 - weight, (count, HS))

    for k in range(kv_heads):
        merge_head(old_ref, share, put, steps, per_kv, k)
    for k in range(kv_heads):
        into(k).wait()
        for s in range(steps):
            for q in range(per_kv):
                h, lanes = k * per_kv + q, pl.ds(q * HS, HS)
                new = arrived[k, s, 0, :, lanes].astype(jnp.float32)
                merged[k, s, 0, :, lanes] = (weighted[s, h] + weights[s, h] * new).astype(
                    jnp.bfloat16
                )
        outof(k).start()
    for k in range(kv_heads):
        outof(k).wait()


def per_device(
    kv_weight, kv_bias, hidden_in, queries, res_cache, res_len, long_cache, long_len, long_dest
):
    step_count, _, serve_rows, width_part = hidden_in.shape
    kv_cols = kv_bias.shape[0]
    kv_heads = kv_cols // (2 * HS)
    query_cols = queries.shape[3]
    head_count = query_cols // HS
    per_kv = head_count // kv_heads
    staying = res_cache.shape[1]
    moving = serve_rows - staying
    rows = head_count * step_count
    tp_size = lax.axis_size("tp")
    tp_index = lax.axis_index("tp")
    group_index = lax.axis_index("grp")
    asked = lax.all_to_all(
        turn(queries, staying, kv_heads), "grp", split_axis=0, concat_axis=0, tiled=True
    )

    flat_hidden = hidden_in.reshape(step_count * serve_rows, width_part)
    pieces = project(flat_hidden, kv_weight, kv_cols, tp_size, tp_index, 1, tp_size - 1)
    others = jnp.stack(
        [
            lax.ppermute(pieces[j], "tp", [(i, (i + j + 1) % tp_size) for i in range(tp_size)])
            for j in range(tp_size - 1)
        ]
    )
    mine = project(flat_hidden, kv_weight, kv_cols, tp_size, tp_index, 0, 1)[0]

    answer = old_call(
        functools.partial(moving_kernel, kv_heads=kv_heads),
        [long_dest, long_len],
        pltpu.HBM,
        asked,
        long_cache[0],
        rows,
        [
            pltpu.SMEM(long_dest.shape, jnp.int32),
            pltpu.SMEM(long_len.shape, jnp.int32),
            pltpu.SMEM((moving + 8,), jnp.int32),
            pltpu.VMEM((moving, rows + STAT, HS), jnp.bfloat16),
            pltpu.SemaphoreType.DMA((2, moving)),
            pltpu.SemaphoreType.DMA((moving,)),
            pltpu.SemaphoreType.DMA((2,)),
        ],
        pltpu.HBM,
        48 * MIB,
        "moving_old",
    )
    answer, others, mine = lax.optimization_barrier((answer, others, mine))
    answer = lax.all_to_all(answer, "grp", split_axis=0, concat_axis=0, tiled=True)

    own_len = res_len[0]
    stayed = old_call(
        functools.partial(staying_kernel, kv_heads=kv_heads),
        [own_len],
        pltpu.SMEM,
        queries,
        res_cache[0],
        rows,
        [pltpu.VMEM((staying, rows, HS), jnp.bfloat16), pltpu.SemaphoreType.DMA((2, staying))],
        pltpu.VMEM,
        58 * MIB,
        "staying_old",
    )
    matched = (long_dest == group_index).astype(jnp.int32)
    len_in = jnp.sum(matched * long_len, axis=1)
    served_len = jnp.concatenate([own_len, len_in])
    positions = served_len[None, :] + jnp.arange(step_count, dtype=jnp.int32)[:, None]
    half = HS // 2
    freqs = jnp.power(jnp.float32(ROPE_BASE), -2.0 * jnp.arange(half, dtype=jnp.float32) / HS)
    angles = positions.reshape(-1, 1).astype(jnp.float32) * freqs
    cosine, sine = jnp.cos(angles), jnp.sin(angles)
    cosine = jnp.concatenate([cosine, cosine], 1)
    sine = jnp.concatenate([-sine, sine], 1)

    out_shape = jax.ShapeDtypeStruct((step_count, 1, serve_rows, query_cols), jnp.bfloat16)
    fresh, lse = pl.pallas_call(
        functools.partial(new_kernel, kv_heads=kv_heads, per_kv=per_kv, staying=staying),
        out_shape=(out_shape, jax.ShapeDtypeStruct((serve_rows, HS), jnp.float32)),
        in_specs=[pl.BlockSpec(memory_space=pltpu.VMEM)] * 7,
        out_specs=(pl.BlockSpec(memory_space=pltpu.VMEM),) * 2,
        compiler_params=pltpu.CompilerParams(vmem_limit_bytes=24 * MIB),
        cost_estimate=pl.CostEstimate(
            flops=serve_rows * rows * step_count * serve_rows * HS * 4,
            bytes_accessed=8 * MIB,
            transcendentals=serve_rows * rows * step_count * serve_rows,
        ),
        name="new_part",
    )(queries, mine, others, kv_bias.reshape(1, kv_cols), cosine, sine, stayed)

    hbm, vmem = pl.BlockSpec(memory_space=pltpu.HBM), pl.BlockSpec(memory_space=pltpu.VMEM)
    part = (kv_heads, step_count, 1, moving, query_cols // kv_heads)
    return pl.pallas_call(
        functools.partial(join_kernel, kv_heads=kv_heads, first=staying),
        out_shape=out_shape,
        in_specs=[vmem, hbm, vmem],
        out_specs=hbm,
        scratch_shapes=[
            pltpu.VMEM(part, jnp.bfloat16),
            pltpu.VMEM((step_count, head_count, moving, HS), jnp.float32),
            pltpu.VMEM((step_count, head_count, moving, HS), jnp.float32),
            pltpu.VMEM(part, jnp.bfloat16),
            pltpu.SemaphoreType.DMA((kv_heads,)),
            pltpu.SemaphoreType.DMA((kv_heads,)),
        ],
        input_output_aliases={1: 0},
        compiler_params=pltpu.CompilerParams(vmem_limit_bytes=32 * MIB),
        cost_estimate=pl.CostEstimate(flops=MIB, bytes_accessed=2 * MIB, transcendentals=0),
        name="join",
    )(answer, fresh, lse)


def solution(mesh):
    placed = (
        P("tp", None),
        P("tp"),
        P(None, "grp", None, "tp"),
        P(None, "grp", None, "tp"),
        P("grp", None, None, "tp"),
        P("grp", None),
        P("grp", None, None, "tp"),
        P(),
        P(),
    )
    return jax.shard_map(
        per_device,
        mesh=mesh,
        in_specs=placed,
        out_specs=P(None, "grp", None, "tp"),
        check_vma=False,
    )
```

```python
import functools
import math

import jax
import jax.numpy as jnp
from jax import lax
from jax.experimental import pallas as pl
from jax.experimental.pallas import tpu as pltpu
from jax.sharding import PartitionSpec as P

HS = 128
ROPE_BASE = 1000000.0
masked_score = -1e30
SCALE = HS ** (-0.5)
LOG2E = math.log2(math.e)
STAT = 8
GROUP = 4
MIB = 1 << 20
FULL = 60 * MIB


def cache_copy(cache_ref, buf, sems, m, begin, end):
    part = pl.ds(begin, end - begin)
    sem = sems.at[0 if begin == 0 else 1, m]
    return pltpu.make_async_copy(cache_ref.at[m, part], buf.at[m, part], sem)


def moving_kernel(
    dest_hbm, length_hbm, query_ref, cache_ref, out_ref,
    buf, dest_ref, length_ref, order, answers, in_sems, out_sems, table_sems, *, kv_heads,
):
    count, capacity, _ = cache_ref.shape
    me = lax.axis_index("grp")
    chunk = min(capacity, 128)
    variants = capacity // chunk
    tables = [
        pltpu.make_async_copy(length_hbm, length_ref, table_sems.at[0]),
        pltpu.make_async_copy(dest_hbm, dest_ref, table_sems.at[1]),
    ]
    for table in tables:
        table.start()
    for m in range(count):
        cache_copy(cache_ref, buf, in_sems, m, 0, chunk).start()
    for table in tables:
        table.wait()
    used = [(length_ref[me, m] + chunk - 1) // chunk for m in range(count)]
    place = jnp.int32(0)
    for v in range(1, variants + 1):
        order[count + v] = place
        place = place + sum((u == v).astype(jnp.int32) for u in used)
    for m in range(count):
        at = order[count + used[m]]
        order[count + used[m]] = at + 1
        order[at] = m

    def leave(slot):
        return pltpu.make_async_copy(answers.at[slot], out_ref.at[slot], out_sems.at[slot])

    old_body(
        lambda m: dest_ref[me, m],
        lambda i: order[i],
        lambda m: length_ref[me, m],
        lambda slot, begin, end: query_ref[slot, begin:end, :],
        cache_ref, answers, buf, in_sems, kv_heads, lambda slot: leave(slot).start(),
    )

    @pl.loop(0, count)
    def _(slot):
        leave(slot).wait()


def staying_kernel(len_ref, query_ref, cache_ref, out_ref, buf, turned, sems, *, kv_heads):
    count, rows = out_ref.shape[0], out_ref.shape[1] - STAT

    steps, per = query_ref.shape[0], rows // kv_heads

    def same(m):
        return m

    for m in range(count):
        cache_copy(cache_ref, buf, sems, m, 0, min(cache_ref.shape[1], 128)).start()

    for k in range(kv_heads):
        turned[:, k * per : (k + 1) * per, :] = by_request(
            lambda s, q: query_ref[s, 0, 0:count, pl.ds((k * per // steps + q) * HS, HS)],
            steps, per // steps,
        )
    old_body(
        same, same, lambda m: len_ref[m], lambda m, begin, end: turned[m, begin:end, :],
        cache_ref, out_ref, buf, sems, kv_heads, lambda slot: None,
    )


def stat_rows(lses):
    rows = lses[0].shape[0]
    same = lax.broadcasted_iota(jnp.int32, (rows, HS), 0) == lax.broadcasted_iota(
        jnp.int32, (rows, HS), 1
    )
    row = lax.broadcasted_iota(jnp.int32, (STAT, HS), 0)
    result = []
    for lse in lses:
        turned = jnp.sum(jnp.where(same, lse, 0.0), axis=0, keepdims=True)
        whole = jnp.broadcast_to(turned, (STAT, HS))
        high = whole.astype(jnp.bfloat16).astype(jnp.float32)
        rest = whole - high
        middle = rest.astype(jnp.bfloat16).astype(jnp.float32)
        terms = jnp.where(row == 0, high, jnp.where(row == 1, middle, rest - middle))
        result.append(jnp.where(row < 3, terms, 0.0).astype(jnp.bfloat16))
    return result


def old_body(slot_of, member, length_of, query_of, cache_ref, out_ref, buf, sems, kv_heads, done):
    count, capacity, _ = cache_ref.shape
    rows = out_ref.shape[1] - STAT
    per = rows // kv_heads
    chunk = min(capacity, 128)
    variants = capacity // chunk
    pair = 2 if kv_heads % 2 == 0 else 1

    def run(act):
        @pl.loop(0, count // GROUP)
        def _(g):
            members = [member(g * GROUP + i) for i in range(GROUP)]
            if variants == 1:
                act(members, 1)
                return
            used = (length_of(members[-1]) + chunk - 1) // chunk
            for v in range(1, variants + 1):
                pl.when(used == v)(functools.partial(act, members, v))

    def chunks(m):
        return (length_of(m) + chunk - 1) // chunk

    def rest(members, v, act, unread):
        if v == 1:
            return
        uniform = chunks(members[0]) == v

        @pl.when(uniform)
        def _():
            for m in members:
                act(cache_copy(cache_ref, buf, sems, m, chunk, v * chunk))

        @pl.when(jnp.logical_not(uniform))
        def _():
            for m in members:
                own = chunks(m)

                @pl.loop(1, own)
                def _(c):
                    part = pl.ds(pl.multiple_of(c * chunk, chunk), chunk)
                    act(
                        pltpu.make_async_copy(
                            cache_ref.at[m, part], buf.at[m, part], sems.at[1, m]
                        )
                    )

                pl.loop(own, v)(functools.partial(unread, m))

    def clear(m, c):
        part = pl.ds(pl.multiple_of(c * chunk, chunk), chunk)
        for h in range(kv_heads):
            lanes = pl.ds((2 * h + 1) * HS, HS)
            buf[m, part, lanes] = jnp.zeros((chunk, HS), jnp.bfloat16)

    def start(members, v):
        rest(members, v, lambda c: c.start(), clear)

    def body(members, v):
        size, length = len(members), v * chunk
        for m in members:
            cache_copy(cache_ref, buf, sems, m, 0, chunk).wait()
        rest(members, v, lambda c: c.wait(), lambda m, c: None)
        slots = [slot_of(m) for m in members]
        column = lax.broadcasted_iota(jnp.int32, (pair * per, length), 1)
        part = pl.ds(0, length)
        items = [
            (i, [p * pair + j for j in range(pair)])
            for i in range(size)
            for p in range(kv_heads // pair)
        ]
        queries = []
        for i, heads in items:
            own = [query_of(slots[i], h * per, (h + 1) * per) for h in heads]
            if pair == 2:
                zero = jnp.zeros_like(own[0])
                own = [
                    jnp.concatenate(
                        [jnp.concatenate([own[0], zero], 1), jnp.concatenate([zero, own[1]], 1)], 0
                    )
                ]
            queries.append(own[0])

        def columns(i, heads, shift):
            at = [h * 2 * HS + shift for h in heads]
            return jnp.concatenate([buf[members[i], part, c : c + HS] for c in at], 1)

        scores = [
            lax.dot_general(
                query, columns(i, heads, 0), (((1,), (1,)), ((), ())),
                preferred_element_type=jnp.float32,
            )
            for query, (i, heads) in zip(queries, items)
        ]
        scores = [
            jnp.where(column < length_of(members[i]), x, masked_score)
            for x, (i, _) in zip(scores, items)
        ]
        highest = [jnp.max(x, axis=1, keepdims=True) for x in scores]
        probs = [jnp.exp2((x - h) * (SCALE * LOG2E)) for x, h in zip(scores, highest)]
        total = [jnp.sum(x, axis=1, keepdims=True) for x in probs]
        probs = [x.astype(jnp.bfloat16) for x in probs]
        mixed = [
            jnp.dot(x, columns(i, heads, HS), preferred_element_type=jnp.float32)
            for x, (i, heads) in zip(probs, items)
        ]
        mixed = [x * (1.0 / t) for x, t in zip(mixed, total)]
        lses = [h * SCALE + jnp.log(t) for h, t in zip(highest, total)]
        terms = stat_rows(
            [
                jnp.concatenate([x for x, (o, _) in zip(lses, items) if o == i], 0)
                for i in range(size)
            ]
        )
        for x, (i, heads) in zip(mixed, items):
            for j, h in enumerate(heads):
                out_ref[slots[i], h * per : (h + 1) * per, :] = x[
                    j * per : (j + 1) * per, j * HS : (j + 1) * HS
                ].astype(jnp.bfloat16)
        for i in range(size):
            out_ref[slots[i], rows : rows + STAT, :] = terms[i]
            done(slots[i])

    if variants > 1:
        run(start)
    run(body)


def by_request(tile_of, steps, per_kv):
    tiles = [tile_of(s, q) for s in range(steps) for q in range(per_kv)]
    return jnp.swapaxes(jnp.stack(tiles, 0), 0, 1)


def turn_kernel(query_ref, out_ref, arrived, turned, in_sems, out_sems, *, kv_heads, first):
    count, rows, _ = out_ref.shape
    steps = query_ref.shape[0]
    per = rows // kv_heads
    width = query_ref.shape[3] // kv_heads
    own = pl.ds(first, count)

    def into(k):
        lanes = pl.ds(k * width, width)
        return pltpu.make_async_copy(
            query_ref.at[:, :, own, lanes], arrived.at[k], in_sems.at[k]
        )

    def outof(k):
        return pltpu.make_async_copy(
            turned.at[k], out_ref.at[:, pl.ds(k * per, per), :], out_sems.at[k]
        )

    for k in range(kv_heads):
        into(k).start()
    for k in range(kv_heads):
        into(k).wait()
        turned[k] = by_request(
            lambda s, q: arrived[k, s, 0, :, q * HS : (q + 1) * HS], steps, per // steps
        )
        outof(k).start()
    for k in range(kv_heads):
        outof(k).wait()


def turn(queries, first, kv_heads):
    steps, _, serve, cols = queries.shape
    count, width = serve - first, cols // kv_heads
    per = steps * width // HS
    return pl.pallas_call(
        functools.partial(turn_kernel, kv_heads=kv_heads, first=first),
        out_shape=jax.ShapeDtypeStruct((count, kv_heads * per, HS), jnp.bfloat16),
        in_specs=[pl.BlockSpec(memory_space=pltpu.HBM)],
        out_specs=pl.BlockSpec(memory_space=pltpu.HBM),
        scratch_shapes=[
            pltpu.VMEM((kv_heads, steps, 1, count, width), jnp.bfloat16),
            pltpu.VMEM((kv_heads, count, per, HS), jnp.bfloat16),
            pltpu.SemaphoreType.DMA((kv_heads,)),
            pltpu.SemaphoreType.DMA((kv_heads,)),
        ],
        compiler_params=pltpu.CompilerParams(vmem_limit_bytes=FULL),
        cost_estimate=pl.CostEstimate(flops=MIB, bytes_accessed=MIB, transcendentals=0),
        name="turn",
    )(queries)


def project_kernel(index_ref, hidden_ref, weight_ref, out_ref):
    del index_ref
    out_ref[0] = jnp.dot(hidden_ref[...], weight_ref[...], preferred_element_type=jnp.float32)


def project(hidden, weight, kv_cols, tp_size, tp_index, first, pieces):
    rows, depth = hidden.shape
    width = min(kv_cols, 512)
    blocks = kv_cols // width
    return pl.pallas_call(
        project_kernel,
        out_shape=jax.ShapeDtypeStruct((pieces, rows, kv_cols), jnp.float32),
        grid_spec=pltpu.PrefetchScalarGridSpec(
            num_scalar_prefetch=1,
            grid=(pieces, blocks),
            in_specs=[
                pl.BlockSpec((rows, depth), lambda j, c, index: (0, 0)),
                pl.BlockSpec(
                    (depth, width),
                    lambda j, c, index: (0, lax.rem(index[0] + first + j, tp_size) * blocks + c),
                ),
            ],
            out_specs=pl.BlockSpec((1, rows, width), lambda j, c, index: (j, 0, c)),
        ),
        compiler_params=pltpu.CompilerParams(vmem_limit_bytes=FULL),
        cost_estimate=pl.CostEstimate(
            flops=2 * rows * depth * kv_cols * pieces,
            bytes_accessed=depth * kv_cols * pieces * 2,
            transcendentals=0,
        ),
        name="project",
    )(tp_index.reshape(1), hidden, weight)


def old_call(kernel, scalars, scalar_space, query, cache, rows, scratch, out_space, limit, name):
    count, capacity, _ = cache.shape
    scalar, vmem = pl.BlockSpec(memory_space=scalar_space), pl.BlockSpec(memory_space=pltpu.VMEM)
    return pl.pallas_call(
        kernel,
        out_shape=jax.ShapeDtypeStruct((count, rows + STAT, HS), jnp.bfloat16),
        in_specs=[scalar] * len(scalars) + [vmem, pl.BlockSpec(memory_space=pltpu.HBM)],
        out_specs=pl.BlockSpec(memory_space=out_space),
        scratch_shapes=[pltpu.VMEM(cache.shape, jnp.bfloat16)] + scratch,
        compiler_params=pltpu.CompilerParams(vmem_limit_bytes=limit),
        cost_estimate=pl.CostEstimate(
            flops=count * rows * capacity * HS * 8,
            bytes_accessed=cache.size * 2,
            transcendentals=count * rows * capacity,
        ),
        name=name,
    )(*scalars, query, cache)


def old_lse(stat):
    return stat[:, 0, :] + stat[:, 1, :] + stat[:, 2, :]


def merge_head(old_ref, share, put, steps, per_kv, k):
    per = steps * per_kv
    old = jnp.swapaxes(old_ref[:, k * per : (k + 1) * per, :], 0, 1).astype(jnp.float32)
    for s in range(steps):
        for q in range(per_kv):
            at = s * per_kv + q
            c = k * per + at
            put(s, k * per_kv + q, share[:, c : c + 1] * old[at], share[:, c : c + 1])


def new_kernel(
    query_ref, mine_ref, other_ref, bias_ref, cos_ref, sin_ref, old_ref, out_ref, lse_ref,
    *, kv_heads, per_kv, staying,
):
    steps, _, serve, _ = query_ref.shape
    rows = old_ref.shape[1] - STAT
    raw = mine_ref[...]
    for i in range(other_ref.shape[0]):
        raw = raw + other_ref[i]
    raw = raw + bias_ref[...].astype(jnp.float32)
    total_rows = steps * serve
    request = lax.broadcasted_iota(jnp.int32, (serve, total_rows), 0)
    column = lax.broadcasted_iota(jnp.int32, (serve, total_rows), 1)
    lane = lax.broadcasted_iota(jnp.int32, (serve, HS), 1)
    lse_all = jnp.zeros((serve, HS), jnp.float32)
    for k in range(kv_heads):
        keys = raw[:, k * 2 * HS : k * 2 * HS + HS]
        keys = keys * cos_ref[...] + pltpu.roll(keys, HS // 2, 1) * sin_ref[...]
        keys = keys.astype(jnp.bfloat16)
        values = raw[:, k * 2 * HS + HS : (k + 1) * 2 * HS].astype(jnp.bfloat16)
        for s in range(steps):
            heads = [k * per_kv + q for q in range(per_kv)]
            query = jnp.concatenate([query_ref[s, 0, :, h * HS : (h + 1) * HS] for h in heads], 0)
            scores = lax.dot_general(
                query, keys, (((1,), (1,)), ((), ())), preferred_element_type=jnp.float32
            )
            seen = column == request
            for t in range(1, s + 1):
                seen = seen | (column == request + t * serve)
            scores = jnp.where(jnp.concatenate([seen] * per_kv, 0), scores, masked_score)
            highest = jnp.max(scores, axis=1, keepdims=True)
            probs = jnp.exp2((scores - highest) * (SCALE * LOG2E))
            total = jnp.sum(probs, axis=1, keepdims=True)
            mixed = jnp.dot(probs.astype(jnp.bfloat16), values, preferred_element_type=jnp.float32)
            mixed = mixed * (1.0 / total)
            lse = highest * SCALE + jnp.log(total)
            for q, h in enumerate(heads):
                c = (k * steps + s) * per_kv + q
                lse_all = jnp.where(lane == c, lse[q * serve : (q + 1) * serve], lse_all)
                out_ref[s, 0, :, h * HS : (h + 1) * HS] = mixed[
                    q * serve : (q + 1) * serve
                ].astype(jnp.bfloat16)
    lse_ref[...] = lse_all

    def put(s, h, old, weight):
        lanes = pl.ds(h * HS, HS)
        new = out_ref[s, 0, 0:staying, lanes].astype(jnp.float32)
        out_ref[s, 0, 0:staying, lanes] = (old + (1.0 - weight) * new).astype(jnp.bfloat16)

    stat = old_lse(old_ref[:, rows : rows + STAT, :].astype(jnp.float32))
    share = 1.0 / (1.0 + jnp.exp(lse_all[0:staying] - stat))
    for k in range(kv_heads):
        merge_head(old_ref, share, put, steps, per_kv, k)


def join_kernel(
    old_ref, new_ref, lse_ref, out_ref, arrived, weighted, weights, merged, in_sems, out_sems,
    *, kv_heads, first,
):
    steps = new_ref.shape[0]
    count, rows = old_ref.shape[0], old_ref.shape[1] - STAT
    width = new_ref.shape[3] // kv_heads
    per_kv = width // HS
    own = pl.ds(first, count)

    def into(k):
        lanes = pl.ds(k * width, width)
        return pltpu.make_async_copy(new_ref.at[:, :, own, lanes], arrived.at[k], in_sems.at[k])

    def outof(k):
        lanes = pl.ds(k * width, width)
        return pltpu.make_async_copy(merged.at[k], out_ref.at[:, :, own, lanes], out_sems.at[k])

    for k in range(kv_heads):
        into(k).start()
    stat = old_lse(old_ref[:, rows : rows + STAT, :].astype(jnp.float32))
    share = 1.0 / (1.0 + jnp.exp(lse_ref[first : first + count, :] - stat))

    def put(s, h, old, weight):
        weighted[s, h] = old
        weights[s, h] = jnp.broadcast_to(1.0 - weight, (count, HS))

    for k in range(kv_heads):
        merge_head(old_ref, share, put, steps, per_kv, k)
    for k in range(kv_heads):
        into(k).wait()
        for s in range(steps):
            for q in range(per_kv):
                h, lanes = k * per_kv + q, pl.ds(q * HS, HS)
                new = arrived[k, s, 0, :, lanes].astype(jnp.float32)
                merged[k, s, 0, :, lanes] = (weighted[s, h] + weights[s, h] * new).astype(
                    jnp.bfloat16
                )
        outof(k).start()
    for k in range(kv_heads):
        outof(k).wait()


def per_device(
    kv_weight, kv_bias, hidden_in, queries, res_cache, res_len, long_cache, long_len, long_dest
):
    step_count, _, serve_rows, width_part = hidden_in.shape
    kv_cols = kv_bias.shape[0]
    kv_heads = kv_cols // (2 * HS)
    query_cols = queries.shape[3]
    head_count = query_cols // HS
    per_kv = head_count // kv_heads
    staying = res_cache.shape[1]
    moving = serve_rows - staying
    rows = head_count * step_count
    tp_size = lax.axis_size("tp")
    tp_index = lax.axis_index("tp")
    group_index = lax.axis_index("grp")
    asked = lax.all_to_all(
        turn(queries, staying, kv_heads), "grp", split_axis=0, concat_axis=0, tiled=True
    )

    flat_hidden = hidden_in.reshape(step_count * serve_rows, width_part)
    pieces = project(flat_hidden, kv_weight, kv_cols, tp_size, tp_index, 1, tp_size - 1)
    others = jnp.stack(
        [
            lax.ppermute(pieces[j], "tp", [(i, (i + j + 1) % tp_size) for i in range(tp_size)])
            for j in range(tp_size - 1)
        ]
    )
    mine = project(flat_hidden, kv_weight, kv_cols, tp_size, tp_index, 0, 1)[0]

    answer = old_call(
        functools.partial(moving_kernel, kv_heads=kv_heads),
        [long_dest, long_len],
        pltpu.HBM,
        asked,
        long_cache[0],
        rows,
        [
            pltpu.SMEM(long_dest.shape, jnp.int32),
            pltpu.SMEM(long_len.shape, jnp.int32),
            pltpu.SMEM((moving + 8,), jnp.int32),
            pltpu.VMEM((moving, rows + STAT, HS), jnp.bfloat16),
            pltpu.SemaphoreType.DMA((2, moving)),
            pltpu.SemaphoreType.DMA((moving,)),
            pltpu.SemaphoreType.DMA((2,)),
        ],
        pltpu.HBM,
        48 * MIB,
        "moving_old",
    )
    answer, others, mine = lax.optimization_barrier((answer, others, mine))
    answer = lax.all_to_all(answer, "grp", split_axis=0, concat_axis=0, tiled=True)

    own_len = res_len[0]
    stayed = old_call(
        functools.partial(staying_kernel, kv_heads=kv_heads),
        [own_len],
        pltpu.SMEM,
        queries,
        res_cache[0],
        rows,
        [pltpu.VMEM((staying, rows, HS), jnp.bfloat16), pltpu.SemaphoreType.DMA((2, staying))],
        pltpu.VMEM,
        58 * MIB,
        "staying_old",
    )
    matched = (long_dest == group_index).astype(jnp.int32)
    len_in = jnp.sum(matched * long_len, axis=1)
    served_len = jnp.concatenate([own_len, len_in])
    positions = served_len[None, :] + jnp.arange(step_count, dtype=jnp.int32)[:, None]
    half = HS // 2
    freqs = jnp.power(jnp.float32(ROPE_BASE), -2.0 * jnp.arange(half, dtype=jnp.float32) / HS)
    angles = positions.reshape(-1, 1).astype(jnp.float32) * freqs
    cosine, sine = jnp.cos(angles), jnp.sin(angles)
    cosine = jnp.concatenate([cosine, cosine], 1)
    sine = jnp.concatenate([-sine, sine], 1)

    out_shape = jax.ShapeDtypeStruct((step_count, 1, serve_rows, query_cols), jnp.bfloat16)
    fresh, lse = pl.pallas_call(
        functools.partial(new_kernel, kv_heads=kv_heads, per_kv=per_kv, staying=staying),
        out_shape=(out_shape, jax.ShapeDtypeStruct((serve_rows, HS), jnp.float32)),
        in_specs=[pl.BlockSpec(memory_space=pltpu.VMEM)] * 7,
        out_specs=(pl.BlockSpec(memory_space=pltpu.VMEM),) * 2,
        compiler_params=pltpu.CompilerParams(vmem_limit_bytes=24 * MIB),
        cost_estimate=pl.CostEstimate(
            flops=serve_rows * rows * step_count * serve_rows * HS * 4,
            bytes_accessed=8 * MIB,
            transcendentals=serve_rows * rows * step_count * serve_rows,
        ),
        name="new_part",
    )(queries, mine, others, kv_bias.reshape(1, kv_cols), cosine, sine, stayed)

    hbm, vmem = pl.BlockSpec(memory_space=pltpu.HBM), pl.BlockSpec(memory_space=pltpu.VMEM)
    part = (kv_heads, step_count, 1, moving, query_cols // kv_heads)
    return pl.pallas_call(
        functools.partial(join_kernel, kv_heads=kv_heads, first=staying),
        out_shape=out_shape,
        in_specs=[vmem, hbm, vmem],
        out_specs=hbm,
        scratch_shapes=[
            pltpu.VMEM(part, jnp.bfloat16),
            pltpu.VMEM((step_count, head_count, moving, HS), jnp.float32),
            pltpu.VMEM((step_count, head_count, moving, HS), jnp.float32),
            pltpu.VMEM(part, jnp.bfloat16),
            pltpu.SemaphoreType.DMA((kv_heads,)),
            pltpu.SemaphoreType.DMA((kv_heads,)),
        ],
        input_output_aliases={1: 0},
        compiler_params=pltpu.CompilerParams(vmem_limit_bytes=32 * MIB),
        cost_estimate=pl.CostEstimate(flops=MIB, bytes_accessed=2 * MIB, transcendentals=0),
        name="join",
    )(answer, fresh, lse)


def solution(mesh):
    placed = (
        P("tp", None),
        P("tp"),
        P(None, "grp", None, "tp"),
        P(None, "grp", None, "tp"),
        P("grp", None, None, "tp"),
        P("grp", None),
        P("grp", None, None, "tp"),
        P(),
        P(),
    )
    return jax.shard_map(
        per_device,
        mesh=mesh,
        in_specs=placed,
        out_specs=P(None, "grp", None, "tp"),
        check_vma=False,
    )
```
